32 devices in a mesh: seq: 16 (over z, y, core), head: 2 (over x).
Axes of the slice: x: 2, y: 2, z: 4, core: 2. Of those that a mesh axis runs over, the one named last changes fastest.
Arguments:
- noisy_q: bfloat16 [4160, 3072], P('seq', 'head'), may hold values from -38 to 38
- noisy_k: bfloat16 [4160, 1024], P('seq', 'head'), may hold values from -38 to 38
- noisy_value: bfloat16 [4160, 1024], P('seq', 'head'), may hold values from -6 to 6
- clean_k: bfloat16 [4160, 1024], P('seq', 'head'), may hold values from -38 to 38
- clean_value: bfloat16 [4160, 1024], P('seq', 'head'), may hold values from -6 to 6
- q_gain: float32 [3072], P('head'), may hold values from 0.1 to 1.9
- key_norm_gain: float32 [1024], P('head'), may hold values from 0.1 to 1.9
- out_grad: bfloat16 [4160, 3072], P('seq', 'head'), may hold values from -18 to 18
- window: int32 [8, 2], replicated, may hold values from -1 to 6, as said below
Outputs:
- attn_out: bfloat16 [4160, 3072], P('seq', 'head')
- grad_q: bfloat16 [4160, 3072], P('seq', 'head')
- grad_k: bfloat16 [4160, 1024], P('seq', 'head')
- grad_v: bfloat16 [4160, 1024], P('seq', 'head')
- grad_clean_k: bfloat16 [4160, 1024], P('seq', 'head')
- grad_clean_v: bfloat16 [4160, 1024], P('seq', 'head')
The draws below stay inside these ranges and needn't reach their ends.
Inputs may be any that keep to these rules, and one draw needn't show every extreme that they name: `window`: row c lists, in an order drawn from the seed, the clean stretch c - 1 and one clean stretch from c - 3 to c - 2 that is 0 or later; an entry is -1 where no such stretch exists.
All inputs are finite; a program needn't handle non-finite values.
Results may differ from the reference program's by a relative error of at most 0.04.
Values may be sent and summed in bfloat16 or wider, within the bound.
A program may use at most 64 MiB of HBM per device.

```python
import math
import jax
import jax.numpy as jnp
from jax import lax

HEAD_SIZE = 128
KEY_VALUE_HEADS = 8
GROUP = 3
STRETCH = 520
WINDOW = 3
SLOTS = 2
HQ = 24
NCH = 8
TOKEN_COUNT = 4160


def feature_scales(count, ratio):
    column = jnp.arange(count, dtype=jnp.int32)
    spots = (column * 37 % HEAD_SIZE).astype(jnp.float32) / max(HEAD_SIZE - 1, 1)
    return jnp.exp(math.log(ratio) * (spots - 0.5))


def block_scaled(key, rows_total, cols_total):
    first_key, second_key = jax.random.split(key)
    basis = jax.random.truncated_normal(first_key, -4.0, 4.0, (rows_total, cols_total), jnp.float32)
    ratio = 10.0
    row_scale = jnp.exp(jax.random.uniform(second_key, (rows_total, 1), jnp.float32, math.log(0.3), math.log(3.0)))
    return basis * row_scale * feature_scales(cols_total, ratio)[None, :]


def draw_noisy_q(key, part):
    block_tile = block_scaled(jax.random.fold_in(key, 1), TOKEN_COUNT, HQ * HEAD_SIZE)
    return block_tile.astype(jnp.bfloat16)


def draw_noisy_k(key, part):
    block_tile = block_scaled(jax.random.fold_in(key, 2), TOKEN_COUNT, KEY_VALUE_HEADS * HEAD_SIZE)
    return block_tile.astype(jnp.bfloat16)


def draw_clean_k(key, part):
    return block_scaled(jax.random.fold_in(key, 3), TOKEN_COUNT, KEY_VALUE_HEADS * HEAD_SIZE).astype(jnp.bfloat16)


def draw_window(key, part):
    stretch_ids = jnp.arange(NCH, dtype=jnp.int32)
    first_key, second_key = jax.random.split(jax.random.fold_in(key, 9))
    previous = jnp.where(stretch_ids >= 1, stretch_ids - 1, -1)
    reach_back = jnp.clip(stretch_ids - 1, 1, WINDOW - 1)
    back_by = jax.random.randint(first_key, (NCH,), 0, reach_back)
    other = stretch_ids - 2 - back_by
    other = jnp.where(other >= 0, other, -1)
    flipped = jax.random.randint(second_key, (NCH,), 0, 2)
    first_col = jnp.where(flipped == 1, other, previous)
    second_col = jnp.where(flipped == 1, previous, other)
    return jnp.stack([first_col, second_col], axis=1).astype(jnp.int32)


def level_of(own_key, extent, shards, least, largest):
    loudness = 1.0
    for axis_at, shards_of in shards:
        draws = jax.random.uniform(jax.random.fold_in(jax.random.fold_in(own_key, 6), axis_at), (shards_of,), jnp.float32, least / len(shards), largest / len(shards))
        loudness = loudness * jnp.repeat(jnp.exp(draws), extent[axis_at] // shards_of).reshape((-1,) + (1,) * (len(extent) - 1 - axis_at))
    return loudness


def centred(stream_key, dims, deviation, limit, shards=(), kind=jnp.bfloat16):
    entries = jax.random.normal(stream_key, dims, jnp.float32) * deviation
    if len(shards) > 0:
        entries = level_of(stream_key, dims, shards, -0.22, 0.18) * entries
    return jnp.clip(entries, min=-limit, max=limit).astype(kind)


def setup_inputs(seed: int = 0) -> dict:
    splits = jax.random.split(jax.random.key(seed), 10)
    return {
        "noisy_q": draw_noisy_q(jax.random.fold_in(splits[9], 71), 0),
        "noisy_k": draw_noisy_k(jax.random.fold_in(splits[9], 71), 0),
        "noisy_value": centred(splits[2], (TOKEN_COUNT, KEY_VALUE_HEADS * HEAD_SIZE), 1.0, 6.0, ((0, 16), (1, 2))),
        "clean_k": draw_clean_k(jax.random.fold_in(splits[9], 71), 0),
        "clean_value": centred(splits[4], (TOKEN_COUNT, KEY_VALUE_HEADS * HEAD_SIZE), 1.0, 6.0, ((0, 16), (1, 2))),
        "q_gain": jnp.clip(1.0 + 0.18 * jax.random.normal(splits[5], (HQ * HEAD_SIZE,), jnp.float32), 0.1, 1.9),
        "key_norm_gain": jnp.clip(1.0 + 0.18 * jax.random.normal(splits[6], (KEY_VALUE_HEADS * HEAD_SIZE,), jnp.float32), 0.1, 1.9),
        "out_grad": centred(splits[7], (TOKEN_COUNT, HQ * HEAD_SIZE), 3.0, 18.0, ((0, 16), (1, 2))),
        "window": draw_window(jax.random.fold_in(splits[9], 71), 0),
    }


EPSILON = 1e-06
NEG_FILL = -1e+30

def normalize(raw_rows, gain_vec):
    full_rows = raw_rows.astype(jnp.float32)
    inv_rms = lax.rsqrt(lax.optimization_barrier(jnp.mean(full_rows * full_rows, axis=1, keepdims=True)) + EPSILON)
    return ((full_rows * inv_rms * gain_vec[None, :]).astype(jnp.bfloat16), inv_rms)

def norm_grad(raw_rows, gain_vec, inv_rms, grad_rows):
    full_rows = raw_rows.astype(jnp.float32)
    scaled = grad_rows * gain_vec[None, :]
    inner_sum = lax.optimization_barrier(jnp.mean(scaled * full_rows, axis=1, keepdims=True))
    return (inv_rms * scaled - full_rows * inv_rms * inv_rms * inv_rms * inner_sum).astype(jnp.bfloat16)

def stretch_attention(q_rows, grad_rows, every_key, key_mask):
    score_scale = HEAD_SIZE ** (-0.5)
    out_parts, dq_parts, dk_parts, dv_parts = ([], [], [], [])
    for key_value_head in range(KEY_VALUE_HEADS):
        key_cols = every_key[:, key_value_head * HEAD_SIZE:(key_value_head + 1) * HEAD_SIZE]
        value_columns = every_key[:, (KEY_VALUE_HEADS + key_value_head) * HEAD_SIZE:(KEY_VALUE_HEADS + key_value_head + 1) * HEAD_SIZE]
        first_col = key_value_head * GROUP * HEAD_SIZE
        last_col = (key_value_head + 1) * GROUP * HEAD_SIZE
        query_rows = q_rows[:, first_col:last_col].reshape(-1, HEAD_SIZE)
        out_grads = grad_rows[:, first_col:last_col].reshape(-1, HEAD_SIZE)
        scores = jnp.dot(query_rows, key_cols.T, preferred_element_type=jnp.float32) * score_scale
        scores = jnp.where(key_mask[None, :], scores, NEG_FILL)
        row_max = lax.optimization_barrier(jnp.max(scores, axis=1, keepdims=True))
        weights = jnp.exp(scores - row_max)
        probs = weights / lax.optimization_barrier(jnp.sum(weights, axis=1, keepdims=True))
        probs_low = probs.astype(jnp.bfloat16)
        head_out = jnp.dot(probs_low, value_columns, preferred_element_type=jnp.float32)
        out_parts.append(head_out.astype(jnp.bfloat16).reshape(STRETCH, GROUP * HEAD_SIZE))
        dprobs = jnp.dot(out_grads, value_columns.T, preferred_element_type=jnp.float32)
        row_delta = lax.optimization_barrier(jnp.sum(out_grads.astype(jnp.float32) * head_out, axis=1, keepdims=True))
        dscores = (probs * (dprobs - row_delta) * score_scale).astype(jnp.bfloat16)
        dq_parts.append(jnp.dot(dscores, key_cols, preferred_element_type=jnp.float32).reshape(STRETCH, GROUP * HEAD_SIZE))
        dk_parts.append(jnp.dot(dscores.T, query_rows, preferred_element_type=jnp.float32))
        dv_parts.append(jnp.dot(probs_low.T, out_grads, preferred_element_type=jnp.float32))
    return (jnp.concatenate(out_parts, axis=1), jnp.concatenate(dq_parts, axis=1), jnp.concatenate(dk_parts + dv_parts, axis=1))

def reference(noisy_q, noisy_k, noisy_value, clean_k, clean_value, q_gain, key_norm_gain, out_grad, window):
    q_norm, q_inv = normalize(noisy_q, q_gain)
    k_norm, k_inv = normalize(noisy_k, key_norm_gain)
    c_norm, c_inv = normalize(clean_k, key_norm_gain)
    noisy_kv = jnp.concatenate([k_norm, noisy_value], axis=1)
    clean_kv = jnp.concatenate([c_norm, clean_value], axis=1)
    kv_width = noisy_kv.shape[1]

    def stretch_step(clean_acc, stretch_id):
        begin_row = (stretch_id * STRETCH).astype(jnp.int32)
        q_rows = lax.dynamic_slice_in_dim(q_norm, begin_row, STRETCH, 0)
        grad_rows = lax.dynamic_slice_in_dim(out_grad, begin_row, STRETCH, 0)
        blocks = [lax.dynamic_slice_in_dim(noisy_kv, begin_row, STRETCH, 0)]
        mask_parts = [jnp.ones((STRETCH,), dtype=bool)]
        listed = window[stretch_id]
        starts = []
        flags = []
        for j in range(SLOTS):
            is_listed = listed[j] >= 0
            start_row = (jnp.maximum(listed[j], 0) * STRETCH).astype(jnp.int32)
            blocks.append(lax.dynamic_slice_in_dim(clean_kv, start_row, STRETCH, 0))
            mask_parts.append(jnp.broadcast_to(is_listed, (STRETCH,)))
            starts.append(start_row)
            flags.append(is_listed)
        out_rows, dq_rows, dkv_rows = stretch_attention(q_rows, grad_rows, jnp.concatenate(blocks, axis=0), jnp.concatenate(mask_parts, axis=0))
        for j in range(SLOTS):
            current = lax.dynamic_slice_in_dim(clean_acc, starts[j], STRETCH, 0)
            added = jnp.where(flags[j], dkv_rows[(1 + j) * STRETCH:(2 + j) * STRETCH], jnp.float32(0.0))
            clean_acc = lax.dynamic_update_slice_in_dim(clean_acc, current + added, starts[j], 0)
        return (clean_acc, (out_rows, dq_rows, dkv_rows[:STRETCH]))
    init_acc = jnp.zeros((NCH * STRETCH, kv_width), dtype=jnp.float32)
    clean_grad, (out_all, dq_all, noisy_grad) = lax.scan(stretch_step, init_acc, jnp.arange(NCH, dtype=jnp.int32))
    attn_out = out_all.reshape(NCH * STRETCH, HQ * HEAD_SIZE)
    dq_norm = dq_all.reshape(NCH * STRETCH, HQ * HEAD_SIZE)
    noisy_grad = noisy_grad.reshape(NCH * STRETCH, kv_width)
    key_columns = KEY_VALUE_HEADS * HEAD_SIZE
    grad_q = norm_grad(noisy_q, q_gain, q_inv, dq_norm)
    grad_k = norm_grad(noisy_k, key_norm_gain, k_inv, noisy_grad[:, :key_columns])
    grad_v = noisy_grad[:, key_columns:].astype(jnp.bfloat16)
    grad_clean_k = norm_grad(clean_k, key_norm_gain, c_inv, clean_grad[:, :key_columns])
    grad_clean_v = clean_grad[:, key_columns:].astype(jnp.bfloat16)
    return (attn_out, grad_q, grad_k, grad_v, grad_clean_k, grad_clean_v)
```

```python
import functools
import math

import jax
import jax.numpy as jnp
from jax import lax
from jax.experimental import pallas as pl
from jax.experimental.pallas import tpu as pltpu
from jax.sharding import PartitionSpec as P

HEAD_SIZE = 128
KEY_VALUE_HEADS = 8
GROUP = 3
STRETCH = 520
WINDOW = 3
SLOTS = 2
HQ = 24

EPSILON = 1e-06
NEG_FILL = -1e30
LOG2E = 1.0 / math.log(2.0)
PIECES = 6


def padded_rows(rows):
    return -(-rows // 16) * 16


def permuted(value, pairs):
    return lax.ppermute(value, "seq", pairs)


def attend_kernel(raw_q, q_inv, gain, grad, bias, *refs):
    kv_refs = refs[:PIECES]
    out_ref, dq_ref = refs[PIECES : PIECES + 2]
    dkv_refs = refs[PIECES + 2 :]
    scale = HEAD_SIZE**-0.5
    keys = jnp.concatenate([ref[0] for ref in kv_refs], axis=0)
    values = jnp.concatenate([ref[1] for ref in kv_refs], axis=0)
    dk_total, dv_total = 0.0, 0.0
    for member in range(GROUP):
        cols = slice(member * HEAD_SIZE, (member + 1) * HEAD_SIZE)
        gain_row = gain[:, cols] * (scale * LOG2E)
        query = (raw_q[:, cols].astype(jnp.float32) * q_inv[...] * gain_row).astype(jnp.bfloat16)
        scores = lax.dot_general(
            query, keys, (((1,), (1,)), ((), ())), preferred_element_type=jnp.float32
        )
        scores = scores + bias[...]
        row_max = jnp.max(scores, axis=1, keepdims=True)
        weights = jnp.exp2(scores - row_max)
        inverse = 1.0 / jnp.sum(weights, axis=1, keepdims=True)
        weights_low = weights.astype(jnp.bfloat16)
        head_out = jnp.dot(weights_low, values, preferred_element_type=jnp.float32) * inverse
        out_ref[:, cols] = head_out.astype(out_ref.dtype)
        grad_rows = grad[:, cols].astype(jnp.float32) * inverse
        delta = jnp.sum(grad_rows * head_out, axis=1, keepdims=True)
        grad_low = grad_rows.astype(jnp.bfloat16)
        dprobs = lax.dot_general(
            grad_low, values, (((1,), (1,)), ((), ())), preferred_element_type=jnp.float32
        )
        dscores = (weights * (dprobs - delta)).astype(jnp.bfloat16)
        dq_ref[:, cols] = jnp.dot(dscores, keys, preferred_element_type=jnp.float32) * scale
        dk_total += lax.dot_general(
            dscores, query, (((0,), (0,)), ((), ())), preferred_element_type=jnp.float32
        )
        dv_total += lax.dot_general(
            weights_low, grad_low, (((0,), (0,)), ((), ())), preferred_element_type=jnp.float32
        )
    dk_total = dk_total * (1.0 / LOG2E)
    rows = kv_refs[0].shape[1]
    for index, ref in enumerate(dkv_refs):
        span = slice(index * rows, (index + 1) * rows)
        ref[0] = dk_total[span].astype(ref.dtype)
        ref[1] = dv_total[span].astype(ref.dtype)


def attend(noisy_q, q_inv, q_gain, out_grad, bias, pieces):
    rows, width = noisy_q.shape
    local_kv = width // (GROUP * HEAD_SIZE)
    piece_rows = pieces[0].shape[1]
    key_rows = PIECES * piece_rows
    group_cols = GROUP * HEAD_SIZE
    row_block = pl.BlockSpec((rows, group_cols), lambda j: (0, j))
    piece_block = pl.BlockSpec((2, piece_rows, HEAD_SIZE), lambda j: (0, 0, j))
    whole = lambda shape: pl.BlockSpec(shape, lambda j: (0, 0))
    flops = 2 * 6 * rows * GROUP * local_kv * key_rows * HEAD_SIZE
    return pl.pallas_call(
        attend_kernel,
        grid=(local_kv,),
        in_specs=[
            row_block,
            whole((rows, 1)),
            pl.BlockSpec((1, group_cols), lambda j: (0, j)),
            row_block,
            whole((1, key_rows)),
        ]
        + [piece_block] * PIECES,
        out_specs=[row_block, row_block] + [piece_block] * PIECES,
        out_shape=[
            jax.ShapeDtypeStruct((rows, width), jnp.bfloat16),
            jax.ShapeDtypeStruct((rows, width), jnp.float32),
        ]
        + [
            jax.ShapeDtypeStruct(pieces[0].shape, (jnp.float32, jnp.bfloat16)[i % 2])
            for i in range(PIECES)
        ],
        compiler_params=pltpu.CompilerParams(
            dimension_semantics=("arbitrary",), vmem_limit_bytes=56 * 1024 * 1024
        ),
        cost_estimate=pl.CostEstimate(
            flops=flops,
            bytes_accessed=16 * 1024 * 1024,
            transcendentals=rows * GROUP * local_kv * key_rows,
        ),
    )(noisy_q, q_inv, q_gain[None, :], out_grad, bias, *pieces)


def on_device(
    noisy_q, noisy_k, noisy_value, clean_k, clean_value, q_gain, key_norm_gain, out_grad, window
):
    rows = noisy_q.shape[0]
    count = lax.axis_size("seq")
    span = STRETCH // rows
    assert span == 2
    piece_rows = padded_rows(rows)
    pad = ((0, 0), (0, piece_rows - rows), (0, 0))
    stretch_id = lax.axis_index("seq") // span
    q_full = noisy_q.astype(jnp.float32)
    k_full = noisy_k.astype(jnp.float32)
    c_full = clean_k.astype(jnp.float32)
    totals = lax.psum(
        jnp.stack(
            [
                jnp.sum(q_full * q_full, axis=1),
                jnp.sum(k_full * k_full, axis=1),
                jnp.sum(c_full * c_full, axis=1),
            ]
        ),
        "head",
    )
    q_width = HQ * HEAD_SIZE
    key_width = KEY_VALUE_HEADS * HEAD_SIZE
    q_inv = lax.rsqrt(totals[0] / q_width + EPSILON)[:, None]
    k_inv = lax.rsqrt(totals[1] / key_width + EPSILON)[:, None]
    c_inv = lax.rsqrt(totals[2] / key_width + EPSILON)[:, None]
    k_norm = (k_full * k_inv * key_norm_gain[None, :]).astype(jnp.bfloat16)
    c_norm = (c_full * c_inv * key_norm_gain[None, :]).astype(jnp.bfloat16)
    noisy_own = jnp.pad(jnp.stack([k_norm, noisy_value]), pad)
    clean_own = jnp.pad(jnp.stack([c_norm, clean_value]), pad)

    partner = [(i, i ^ 1) for i in range(count)]
    ahead = lambda steps: [(i, i + steps * span) for i in range(count - steps * span)]
    back = lambda steps: [(i, i - steps * span) for i in range(steps * span, count)]

    ids = jnp.arange(window.shape[0], dtype=jnp.int32)
    low = jnp.min(window, axis=1)
    high = jnp.max(window, axis=1)
    pick = lambda table, at: jnp.sum(jnp.where(ids == at, table, 0))
    has_prev = pick(high, stretch_id) >= 0
    has_other = (pick(low, stretch_id) >= 0) & (pick(low, stretch_id) < pick(high, stretch_id))
    later_takes_own = pick(low, stretch_id + 2) == stretch_id

    prev_own = permuted(clean_own, ahead(1))
    noisy_par = permuted(noisy_own, partner)
    other_own = permuted(jnp.where(later_takes_own, clean_own, prev_own), ahead(2))
    prev_par = permuted(prev_own, partner)
    other_par = permuted(other_own, partner)

    real = jnp.arange(piece_rows) < rows
    flags = [True, True, has_prev, has_prev, has_other, has_other]
    bias = jnp.concatenate([jnp.where(real & flag, 0.0, NEG_FILL) for flag in flags])
    attn_out, dq_norm, dn_own, dn_par, dp_own, dp_par, do_own, do_par = attend(
        noisy_q,
        q_inv,
        q_gain,
        out_grad,
        bias[None, :].astype(jnp.float32),
        [noisy_own, noisy_par, prev_own, prev_par, other_own, other_par],
    )
    do_total = do_own + permuted(do_par, partner)
    dp_total = dp_own + permuted(dp_par, partner)
    dn_total = dn_own + permuted(dn_par, partner)
    from_later = permuted(do_total.astype(jnp.bfloat16), back(2)).astype(jnp.float32)
    dp_total = dp_total + jnp.where(later_takes_own, 0.0, from_later)
    from_next = permuted(dp_total.astype(jnp.bfloat16), back(1)).astype(jnp.float32)
    dc_total = from_next + jnp.where(later_takes_own, from_later, 0.0)

    q_scaled = dq_norm * q_gain[None, :]
    k_scaled = dn_total[0, :rows] * key_norm_gain[None, :]
    c_scaled = dc_total[0, :rows] * key_norm_gain[None, :]
    inner_sum = lax.psum(
        jnp.stack(
            [
                jnp.sum(q_scaled * q_full, axis=1),
                jnp.sum(k_scaled * k_full, axis=1),
                jnp.sum(c_scaled * c_full, axis=1),
            ]
        ),
        "head",
    )

    def norm_grad(full, inv, scaled, inner, width):
        return (inv * scaled - full * inv * inv * inv * (inner / width)[:, None]).astype(
            jnp.bfloat16
        )

    grad_q = norm_grad(q_full, q_inv, q_scaled, inner_sum[0], q_width)
    grad_k = norm_grad(k_full, k_inv, k_scaled, inner_sum[1], key_width)
    grad_clean_k = norm_grad(c_full, c_inv, c_scaled, inner_sum[2], key_width)
    grad_v = dn_total[1, :rows].astype(jnp.bfloat16)
    grad_clean_v = dc_total[1, :rows].astype(jnp.bfloat16)
    return (attn_out, grad_q, grad_k, grad_v, grad_clean_k, grad_clean_v)


def solution(mesh):
    split = P("seq", "head")
    return jax.shard_map(
        on_device,
        mesh=mesh,
        in_specs=(split, split, split, split, split, P("head"), P("head"), split, P()),
        out_specs=(split,) * 6,
        check_vma=False,
    )
```

```python
import math

import jax
import jax.numpy as jnp
from jax import lax
from jax.experimental import pallas as pl
from jax.experimental.pallas import tpu as pltpu
from jax.sharding import PartitionSpec as P

HEAD_SIZE = 128
KEY_VALUE_HEADS = 8
GROUP = 3
STRETCH = 520
WINDOW = 3
SLOTS = 2
HQ = 24

EPSILON = 1e-06
NEG_FILL = -1e30
LOG2E = 1.0 / math.log(2.0)
PIECES = 6


def padded_rows(rows):
    return -(-rows // 16) * 16


def key_pieces(bufs, head, part):
    return jnp.concatenate([buf[head, part] for buf in bufs], axis=0)


def stretch_kernel(
    raw_q,
    q_inv,
    q_gain,
    grad,
    bias,
    raw_k,
    value,
    k_inv,
    raw_c,
    clean_value,
    c_inv,
    key_gain,
    take_own,
    out_ref,
    dq_ref,
    dk_ref,
    dv_ref,
    dck_ref,
    dcv_ref,
    noisy_own,
    clean_own,
    noisy_par,
    prev_own,
    prev_par,
    relay,
    other_own,
    other_par,
    grad_own,
    grad_out,
    grad_in,
    later_out,
    later_in,
    next_out,
    next_in,
    send_sems,
    recv_sems,
):
    heads = noisy_own.shape[0]
    rows = raw_q.shape[0]
    piece_rows = noisy_own.shape[2]
    scale = HEAD_SIZE**-0.5
    here = lax.axis_index("seq")
    count = lax.axis_size("seq")
    partner = here + 1 - 2 * (here % 2)
    ahead = lambda steps: (here + 2 * steps) % count
    back = lambda steps: (here + count - 2 * steps) % count

    barrier = pltpu.get_barrier_semaphore()
    peers = (partner, ahead(1), ahead(2), back(1), back(2))
    for peer in peers:
        pl.semaphore_signal(
            barrier, inc=1, device_id={"seq": peer}, device_id_type=pl.DeviceIdType.MESH
        )

    def copy(kind, head, src, dst, target):
        return pltpu.make_async_remote_copy(
            src_ref=src.at[head],
            dst_ref=dst.at[head],
            send_sem=send_sems.at[kind, head],
            recv_sem=recv_sems.at[kind, head],
            device_id={"seq": target},
            device_id_type=pl.DeviceIdType.MESH,
        )

    clean_next = lambda h: copy(0, h, clean_own, prev_own, ahead(1))
    noisy_pair = lambda h: copy(1, h, noisy_own, noisy_par, partner)
    prev_pair = lambda h: copy(2, h, prev_own, prev_par, partner)
    clean_later = lambda h: copy(3, h, relay, other_own, ahead(2))
    other_pair = lambda h: copy(4, h, other_own, other_par, partner)
    grad_pair = lambda h: copy(5, h, grad_out, grad_in, partner)
    grad_later = lambda h: copy(6, h, later_out, later_in, back(2))
    grad_next = lambda h: copy(7, h, next_out, next_in, back(1))
    kinds = (
        clean_next,
        noisy_pair,
        prev_pair,
        clean_later,
        other_pair,
        grad_pair,
        grad_later,
        grad_next,
    )

    noisy_own[...] = jnp.zeros_like(noisy_own)
    clean_own[...] = jnp.zeros_like(clean_own)
    for h in range(heads):
        cols = slice(h * HEAD_SIZE, (h + 1) * HEAD_SIZE)
        gain_row = key_gain[:, cols]
        clean_own[h, 0, :rows] = (raw_c[:, cols].astype(jnp.float32) * c_inv[...] * gain_row).astype(
            jnp.bfloat16
        )
        clean_own[h, 1, :rows] = clean_value[:, cols]
        if h == 0:
            pl.semaphore_wait(barrier, len(peers))
        if h < 2:
            clean_next(h).start()
        noisy_own[h, 0, :rows] = (raw_k[:, cols].astype(jnp.float32) * k_inv[...] * gain_row).astype(
            jnp.bfloat16
        )
        noisy_own[h, 1, :rows] = value[:, cols]
        noisy_pair(h).start()

    def pass_clean(h):
        clean_next(h).wait_recv()
        prev_pair(h).start()
        own = clean_own[h].astype(jnp.float32)
        prev = prev_own[h].astype(jnp.float32)
        relay[h] = jnp.where(take_own[...] > 0.0, own, prev).astype(jnp.bfloat16)
        clean_later(h).start()

    def pass_other(h):
        clean_later(h).wait_recv()
        other_pair(h).start()

    def pass_grads(h):
        grad_pair(h).wait_recv()
        later_out[h] = (grad_own[h, 2] + grad_in[h, 2].astype(jnp.float32)).astype(jnp.bfloat16)
        grad_later(h).start()
        cols = pl.ds(pl.multiple_of(h * HEAD_SIZE, HEAD_SIZE), HEAD_SIZE)
        total = grad_own[h, 0] + grad_in[h, 0].astype(jnp.float32)
        dk_ref[:, cols] = total[0]
        dv_ref[:, cols] = total[1].astype(jnp.bfloat16)
        grad_own[h, 1] = grad_own[h, 1] + grad_in[h, 1].astype(jnp.float32)

    def pass_later(h):
        grad_later(h).wait_recv()
        arrived = later_in[h].astype(jnp.float32)
        own = take_own[...] > 0.0
        next_out[h] = (grad_own[h, 1] + jnp.where(own, 0.0, arrived)).astype(jnp.bfloat16)
        grad_next(h).start()

    def finish(h):
        grad_next(h).wait_recv()
        own = take_own[...] > 0.0
        total = next_in[h].astype(jnp.float32) + jnp.where(
            own, later_in[h].astype(jnp.float32), 0.0
        )
        cols = pl.ds(pl.multiple_of(h * HEAD_SIZE, HEAD_SIZE), HEAD_SIZE)
        dck_ref[:, cols] = total[0]
        dcv_ref[:, cols] = total[1].astype(jnp.bfloat16)

    for h in range(min(2, heads)):
        pass_clean(h)
        if h + 2 < heads:
            clean_next(h + 2).start()
    pass_other(0)

    own_par = (noisy_own, noisy_par, prev_own, prev_par, other_own, other_par)

    def step(h, carry):
        noisy_pair(h).wait_recv()
        prev_pair(h).wait_recv()
        other_pair(h).wait_recv()
        keys = key_pieces(own_par, h, 0)
        values = key_pieces(own_par, h, 1)
        dk_total, dv_total = 0.0, 0.0
        for member in range(GROUP):
            first = pl.multiple_of((h * GROUP + member) * HEAD_SIZE, HEAD_SIZE)
            cols = pl.ds(first, HEAD_SIZE)
            gain_row = q_gain[:, cols] * (scale * LOG2E)
            query = (raw_q[:, cols].astype(jnp.float32) * q_inv[...] * gain_row).astype(
                jnp.bfloat16
            )
            scores = lax.dot_general(
                query, keys, (((1,), (1,)), ((), ())), preferred_element_type=jnp.float32
            )
            scores = scores + bias[...]
            row_max = jnp.max(scores, axis=1, keepdims=True)
            weights = jnp.exp2(scores - row_max)
            inverse = 1.0 / jnp.sum(weights, axis=1, keepdims=True)
            weights_low = weights.astype(jnp.bfloat16)
            head_out = jnp.dot(weights_low, values, preferred_element_type=jnp.float32) * inverse
            out_ref[:, cols] = head_out.astype(out_ref.dtype)
            grad_rows = grad[:, cols].astype(jnp.float32) * inverse
            delta = jnp.sum(grad_rows * head_out, axis=1, keepdims=True)
            grad_low = grad_rows.astype(jnp.bfloat16)
            dprobs = lax.dot_general(
                grad_low, values, (((1,), (1,)), ((), ())), preferred_element_type=jnp.float32
            )
            dscores = (weights * (dprobs - delta)).astype(jnp.bfloat16)
            dq_ref[:, cols] = jnp.dot(dscores, keys, preferred_element_type=jnp.float32) * scale
            dk_total += lax.dot_general(
                dscores, query, (((0,), (0,)), ((), ())), preferred_element_type=jnp.float32
            )
            dv_total += lax.dot_general(
                weights_low, grad_low, (((0,), (0,)), ((), ())), preferred_element_type=jnp.float32
            )
            if member == 0:
                pl.when(h + 2 < heads)(lambda: pass_clean(h + 2))
                pl.when(h >= 1)(lambda: pass_grads(h - 1))
            if member == 1:
                pl.when(h + 1 < heads)(lambda: pass_other(h + 1))
                pl.when(h >= 2)(lambda: pass_later(h - 2))
        dk_total = dk_total * (1.0 / LOG2E)
        for index in range(PIECES // 2):
            for part, total in enumerate((dk_total, dv_total)):
                at = 2 * index * piece_rows
                grad_own[h, index, part] = total[at : at + piece_rows]
                grad_out[h, index, part] = total[at + piece_rows : at + 2 * piece_rows].astype(
                    jnp.bfloat16
                )
        grad_pair(h).start()
        return carry

    lax.fori_loop(0, heads, step, 0)
    pass_grads(heads - 1)
    for h in range(max(heads - 2, 0), heads):
        pass_later(h)
    for h in range(heads):
        finish(h)
    for kind in kinds:
        for h in range(heads):
            kind(h).wait_send()


def attend(raw_q, q_inv, q_gain, grad, bias, raw_k, value, k_inv, raw_c, clean_value, c_inv, key_gain, take_own):
    rows, width = raw_q.shape
    heads = raw_k.shape[1] // HEAD_SIZE
    piece_rows = padded_rows(rows)
    key_rows = PIECES * piece_rows
    piece = pltpu.VMEM((heads, 2, piece_rows, HEAD_SIZE), jnp.bfloat16)
    triple = (heads, 3, 2, piece_rows, HEAD_SIZE)
    key_out = (piece_rows, heads * HEAD_SIZE)
    args = (
        raw_q,
        q_inv,
        q_gain[None, :],
        grad,
        bias,
        raw_k,
        value,
        k_inv,
        raw_c,
        clean_value,
        c_inv,
        key_gain[None, :],
        take_own,
    )
    vmem = pl.BlockSpec(memory_space=pltpu.VMEM)
    return pl.pallas_call(
        stretch_kernel,
        in_specs=[vmem] * len(args),
        out_specs=[vmem] * 6,
        out_shape=[
            jax.ShapeDtypeStruct((rows, width), jnp.bfloat16),
            jax.ShapeDtypeStruct((rows, width), jnp.float32),
            jax.ShapeDtypeStruct(key_out, jnp.float32),
            jax.ShapeDtypeStruct(key_out, jnp.bfloat16),
            jax.ShapeDtypeStruct(key_out, jnp.float32),
            jax.ShapeDtypeStruct(key_out, jnp.bfloat16),
        ],
        scratch_shapes=[piece] * 8
        + [
            pltpu.VMEM(triple, jnp.float32),
            pltpu.VMEM(triple, jnp.bfloat16),
            pltpu.VMEM(triple, jnp.bfloat16),
        ]
        + [piece] * 4
        + [pltpu.SemaphoreType.DMA((8, heads)), pltpu.SemaphoreType.DMA((8, heads))],
        compiler_params=pltpu.CompilerParams(
            collective_id=0, has_side_effects=True, vmem_limit_bytes=58 * 1024 * 1024
        ),
        cost_estimate=pl.CostEstimate(
            flops=2 * 6 * rows * GROUP * heads * key_rows * HEAD_SIZE,
            bytes_accessed=16 * 1024 * 1024,
            transcendentals=rows * GROUP * heads * key_rows,
        ),
    )(*args)


def on_device(
    noisy_q, noisy_k, noisy_value, clean_k, clean_value, q_gain, key_norm_gain, out_grad, window
):
    rows = noisy_q.shape[0]
    span = STRETCH // rows
    assert span == 2
    piece_rows = padded_rows(rows)
    stretch_id = lax.axis_index("seq") // span
    q_full = noisy_q.astype(jnp.float32)
    k_full = noisy_k.astype(jnp.float32)
    c_full = clean_k.astype(jnp.float32)
    totals = lax.psum(
        jnp.stack(
            [
                jnp.sum(q_full * q_full, axis=1),
                jnp.sum(k_full * k_full, axis=1),
                jnp.sum(c_full * c_full, axis=1),
            ]
        ),
        "head",
    )
    q_width = HQ * HEAD_SIZE
    key_width = KEY_VALUE_HEADS * HEAD_SIZE
    q_inv = lax.rsqrt(totals[0] / q_width + EPSILON)[:, None]
    k_inv = lax.rsqrt(totals[1] / key_width + EPSILON)[:, None]
    c_inv = lax.rsqrt(totals[2] / key_width + EPSILON)[:, None]

    ids = jnp.arange(window.shape[0], dtype=jnp.int32)
    low = jnp.min(window, axis=1)
    high = jnp.max(window, axis=1)
    pick = lambda table, at: jnp.sum(jnp.where(ids == at, table, 0))
    has_prev = pick(high, stretch_id) >= 0
    has_other = (pick(low, stretch_id) >= 0) & (pick(low, stretch_id) < pick(high, stretch_id))
    later_takes_own = pick(low, stretch_id + 2) == stretch_id

    real = jnp.arange(piece_rows) < rows
    flags = [True, True, has_prev, has_prev, has_other, has_other]
    bias = jnp.concatenate([jnp.where(real & flag, 0.0, NEG_FILL) for flag in flags])
    attn_out, dq_norm, dk_norm, grad_v, dc_norm, grad_clean_v = attend(
        noisy_q,
        q_inv,
        q_gain,
        out_grad,
        bias[None, :].astype(jnp.float32),
        noisy_k,
        noisy_value,
        k_inv,
        clean_k,
        clean_value,
        c_inv,
        key_norm_gain,
        jnp.full((1, HEAD_SIZE), later_takes_own.astype(jnp.float32)),
    )

    q_scaled = dq_norm * q_gain[None, :]
    k_scaled = dk_norm[:rows] * key_norm_gain[None, :]
    c_scaled = dc_norm[:rows] * key_norm_gain[None, :]
    inner_sum = lax.psum(
        jnp.stack(
            [
                jnp.sum(q_scaled * q_full, axis=1),
                jnp.sum(k_scaled * k_full, axis=1),
                jnp.sum(c_scaled * c_full, axis=1),
            ]
        ),
        "head",
    )

    def norm_grad(full, inv, scaled, inner, width):
        return (inv * scaled - full * inv * inv * inv * (inner / width)[:, None]).astype(
            jnp.bfloat16
        )

    grad_q = norm_grad(q_full, q_inv, q_scaled, inner_sum[0], q_width)
    grad_k = norm_grad(k_full, k_inv, k_scaled, inner_sum[1], key_width)
    grad_clean_k = norm_grad(c_full, c_inv, c_scaled, inner_sum[2], key_width)
    return (attn_out, grad_q, grad_k, grad_v[:rows], grad_clean_k, grad_clean_v[:rows])


def solution(mesh):
    split = P("seq", "head")
    return jax.shard_map(
        on_device,
        mesh=mesh,
        in_specs=(split, split, split, split, split, P("head"), P("head"), split, P()),
        out_specs=(split,) * 6,
        check_vma=False,
    )
```

```python
import math

import jax
import jax.numpy as jnp
from jax import lax
from jax.experimental import pallas as pl
from jax.experimental.pallas import tpu as pltpu
from jax.sharding import PartitionSpec as P

HEAD_SIZE = 128
KEY_VALUE_HEADS = 8
GROUP = 3
STRETCH = 520
WINDOW = 3
SLOTS = 2
HQ = 24

EPSILON = 1e-06
NEG_FILL = -1e30
LOG2E = 1.0 / math.log(2.0)
PIECES = 6


def padded_rows(rows):
    return -(-rows // 16) * 16


def key_pieces(bufs, head, part):
    return jnp.concatenate([buf[head, part] for buf in bufs], axis=0)


def stretch_kernel(
    window,
    raw_q,
    raw_k,
    value,
    raw_c,
    clean_value,
    q_gain,
    key_gain,
    grad,
    out_ref,
    grad_q_ref,
    grad_k_ref,
    grad_v_ref,
    grad_ck_ref,
    grad_cv_ref,
    noisy_own,
    clean_own,
    noisy_par,
    prev_own,
    prev_par,
    relay,
    other_own,
    other_par,
    grad_own,
    grad_out,
    grad_in,
    later_out,
    later_in,
    next_out,
    next_in,
    q_scaled,
    k_scaled,
    c_scaled,
    inner,
    inverse_rms,
    bias,
    take_own,
    stat_out,
    stat_in,
    send_sems,
    recv_sems,
    stat_send,
    stat_recv,
):
    heads = noisy_own.shape[0]
    rows = raw_q.shape[0]
    piece_rows = noisy_own.shape[2]
    scale = HEAD_SIZE**-0.5
    here = lax.axis_index("seq")
    count = lax.axis_size("seq")
    partner = here + 1 - 2 * (here % 2)
    ahead = lambda steps: (here + 2 * steps) % count
    back = lambda steps: (here + count - 2 * steps) % count

    barrier = pltpu.get_barrier_semaphore()
    peers = (partner, ahead(1), ahead(2), back(1), back(2))
    for peer in peers:
        pl.semaphore_signal(
            barrier, inc=1, device_id={"seq": peer}, device_id_type=pl.DeviceIdType.MESH
        )
    side = lax.axis_index("head")
    sides = lax.axis_size("head")
    for step_by in range(1, sides):
        pl.semaphore_signal(
            barrier,
            inc=1,
            device_id={"head": (side + step_by) % sides},
            device_id_type=pl.DeviceIdType.MESH,
        )

    def stat_copy(kind, step_by):
        return pltpu.make_async_remote_copy(
            src_ref=stat_out.at[kind],
            dst_ref=stat_in.at[kind, step_by - 1],
            send_sem=stat_send.at[kind, step_by - 1],
            recv_sem=stat_recv.at[kind, step_by - 1],
            device_id={"head": (side + step_by) % sides},
            device_id_type=pl.DeviceIdType.MESH,
        )

    def share(kind, columns):
        lane = lax.broadcasted_iota(jnp.int32, (rows, HEAD_SIZE), 1)
        packed = jnp.zeros((rows, HEAD_SIZE), jnp.float32)
        for at, column in enumerate(columns):
            packed = jnp.where(lane == at, column, packed)
        stat_out[kind, :rows] = packed
        for step_by in range(1, sides):
            stat_copy(kind, step_by).start()

    def shared(kind):
        total = stat_out[kind]
        for step_by in range(1, sides):
            stat_copy(kind, step_by).wait_recv()
            total = total + stat_in[kind, step_by - 1]
        return total[:rows]

    def square_sum(ref):
        total = jnp.zeros((rows, HEAD_SIZE), jnp.float32)
        for first in range(0, ref.shape[1], HEAD_SIZE):
            full = ref[:, first : first + HEAD_SIZE].astype(jnp.float32)
            total = total + full * full
        return jnp.sum(total, axis=1, keepdims=True)

    q_width = HQ * HEAD_SIZE
    key_width = KEY_VALUE_HEADS * HEAD_SIZE
    stat_out[...] = jnp.zeros_like(stat_out)
    square_sums = [square_sum(ref) for ref in (raw_q, raw_k, raw_c)]
    pl.semaphore_wait(barrier, len(peers) + sides - 1)
    share(0, square_sums)

    stretch_id = here // 2
    later_id = (stretch_id + 2) % window.shape[0]
    first_entry, second_entry = window[stretch_id, 0], window[stretch_id, 1]
    high = jnp.maximum(first_entry, second_entry)
    low = jnp.minimum(first_entry, second_entry)
    later_low = jnp.minimum(window[later_id, 0], window[later_id, 1])
    own_id = jnp.full((1, HEAD_SIZE), stretch_id, jnp.int32)
    take_own[...] = jnp.where(jnp.full((1, HEAD_SIZE), later_low) == own_id, 1.0, 0.0)
    lane = lax.broadcasted_iota(jnp.int32, bias.shape, 1)
    held = jnp.zeros(bias.shape, jnp.float32)
    for index in range(PIECES):
        at = index * piece_rows
        inside = jnp.where((lane >= at) & (lane < at + rows), 1.0, 0.0)
        if index >= 2:
            entry = jnp.full(bias.shape, high if index < 4 else low)
            inside = jnp.where(entry >= 0, inside, 0.0)
        held = held + inside
    bias[...] = jnp.where(held > 0.0, 0.0, NEG_FILL)
    inner[...] = jnp.zeros_like(inner)

    def copy(kind, head, src, dst, target):
        return pltpu.make_async_remote_copy(
            src_ref=src.at[head],
            dst_ref=dst.at[head],
            send_sem=send_sems.at[kind, head],
            recv_sem=recv_sems.at[kind, head],
            device_id={"seq": target},
            device_id_type=pl.DeviceIdType.MESH,
        )

    clean_next = lambda h: copy(0, h, clean_own, prev_own, ahead(1))
    noisy_pair = lambda h: copy(1, h, noisy_own, noisy_par, partner)
    prev_pair = lambda h: copy(2, h, prev_own, prev_par, partner)
    clean_later = lambda h: copy(3, h, relay, other_own, ahead(2))
    other_pair = lambda h: copy(4, h, other_own, other_par, partner)
    grad_pair = lambda h: copy(5, h, grad_out, grad_in, partner)
    grad_later = lambda h: copy(6, h, later_out, later_in, back(2))
    grad_next = lambda h: copy(7, h, next_out, next_in, back(1))
    kinds = (
        clean_next,
        noisy_pair,
        prev_pair,
        clean_later,
        other_pair,
        grad_pair,
        grad_later,
        grad_next,
    )

    noisy_own[...] = jnp.zeros_like(noisy_own)
    clean_own[...] = jnp.zeros_like(clean_own)
    totals = shared(0)
    for at, width in enumerate((q_width, key_width, key_width)):
        mean = totals[:, at : at + 1] * (1.0 / width)
        inverse_rms[at] = jnp.broadcast_to(lax.rsqrt(mean + EPSILON), (rows, HEAD_SIZE))
    for h in range(heads):
        cols = slice(h * HEAD_SIZE, (h + 1) * HEAD_SIZE)
        gain_row = key_gain[:, cols]
        clean_own[h, 0, :rows] = (raw_c[:, cols].astype(jnp.float32) * inverse_rms[2] * gain_row).astype(
            jnp.bfloat16
        )
        clean_own[h, 1, :rows] = clean_value[:, cols]
        if h < 2:
            clean_next(h).start()
        noisy_own[h, 0, :rows] = (raw_k[:, cols].astype(jnp.float32) * inverse_rms[1] * gain_row).astype(
            jnp.bfloat16
        )
        noisy_own[h, 1, :rows] = value[:, cols]
        noisy_pair(h).start()

    def pass_clean(h):
        clean_next(h).wait_recv()
        prev_pair(h).start()
        own = clean_own[h].astype(jnp.float32)
        prev = prev_own[h].astype(jnp.float32)
        relay[h] = jnp.where(take_own[...] > 0.0, own, prev).astype(jnp.bfloat16)
        clean_later(h).start()

    def pass_other(h):
        clean_later(h).wait_recv()
        other_pair(h).start()

    def pass_grads(h):
        grad_pair(h).wait_recv()
        later_out[h] = (grad_own[h, 2] + grad_in[h, 2].astype(jnp.float32)).astype(jnp.bfloat16)
        grad_later(h).start()
        cols = pl.ds(pl.multiple_of(h * HEAD_SIZE, HEAD_SIZE), HEAD_SIZE)
        total = grad_own[h, 0] + grad_in[h, 0].astype(jnp.float32)
        scaled = total[0, :rows] * key_gain[:, cols]
        k_scaled[:, cols] = scaled
        inner[1] += scaled * raw_k[:, cols].astype(jnp.float32)
        grad_v_ref[:, cols] = total[1, :rows].astype(jnp.bfloat16)
        grad_own[h, 1] = grad_own[h, 1] + grad_in[h, 1].astype(jnp.float32)

    def pass_later(h):
        grad_later(h).wait_recv()
        arrived = later_in[h].astype(jnp.float32)
        own = take_own[...] > 0.0
        next_out[h] = (grad_own[h, 1] + jnp.where(own, 0.0, arrived)).astype(jnp.bfloat16)
        grad_next(h).start()

    def finish(h):
        grad_next(h).wait_recv()
        own = take_own[...] > 0.0
        total = next_in[h].astype(jnp.float32) + jnp.where(
            own, later_in[h].astype(jnp.float32), 0.0
        )
        cols = pl.ds(pl.multiple_of(h * HEAD_SIZE, HEAD_SIZE), HEAD_SIZE)
        scaled = total[0, :rows] * key_gain[:, cols]
        c_scaled[:, cols] = scaled
        inner[2] += scaled * raw_c[:, cols].astype(jnp.float32)
        grad_cv_ref[:, cols] = total[1, :rows].astype(jnp.bfloat16)

    def norm_grad(ref, raw, scaled, at, inner_sum, width):
        inv = inverse_rms[at]
        factor = inv * inv * inv * (inner_sum * (1.0 / width))
        for first in range(0, ref.shape[1], HEAD_SIZE):
            cols = slice(first, first + HEAD_SIZE)
            full = raw[:, cols].astype(jnp.float32)
            ref[:, cols] = (inv * scaled[:, cols] - full * factor).astype(ref.dtype)

    for h in range(min(2, heads)):
        pass_clean(h)
        if h + 2 < heads:
            clean_next(h + 2).start()
    pass_other(0)

    own_par = (noisy_own, noisy_par, prev_own, prev_par, other_own, other_par)

    def step(h, carry):
        noisy_pair(h).wait_recv()
        prev_pair(h).wait_recv()
        other_pair(h).wait_recv()
        keys = key_pieces(own_par, h, 0)
        values = key_pieces(own_par, h, 1)
        dk_total, dv_total = 0.0, 0.0
        for member in range(GROUP):
            first = pl.multiple_of((h * GROUP + member) * HEAD_SIZE, HEAD_SIZE)
            cols = pl.ds(first, HEAD_SIZE)
            gain_row = q_gain[:, cols] * (scale * LOG2E)
            query = (raw_q[:, cols].astype(jnp.float32) * inverse_rms[0] * gain_row).astype(
                jnp.bfloat16
            )
            scores = lax.dot_general(
                query, keys, (((1,), (1,)), ((), ())), preferred_element_type=jnp.float32
            )
            scores = scores + bias[...]
            row_max = jnp.max(scores, axis=1, keepdims=True)
            weights = jnp.exp2(scores - row_max)
            inverse = 1.0 / jnp.sum(weights, axis=1, keepdims=True)
            weights_low = weights.astype(jnp.bfloat16)
            head_out = jnp.dot(weights_low, values, preferred_element_type=jnp.float32) * inverse
            out_ref[:, cols] = head_out.astype(out_ref.dtype)
            grad_rows = grad[:, cols].astype(jnp.float32) * inverse
            delta = jnp.sum(grad_rows * head_out, axis=1, keepdims=True)
            grad_low = grad_rows.astype(jnp.bfloat16)
            dprobs = lax.dot_general(
                grad_low, values, (((1,), (1,)), ((), ())), preferred_element_type=jnp.float32
            )
            dscores = (weights * (dprobs - delta)).astype(jnp.bfloat16)
            dq = jnp.dot(dscores, keys, preferred_element_type=jnp.float32)
            scaled = dq * (q_gain[:, cols] * scale)
            q_scaled[:, cols] = scaled
            inner[0] += scaled * raw_q[:, cols].astype(jnp.float32)
            dk_total += lax.dot_general(
                dscores, query, (((0,), (0,)), ((), ())), preferred_element_type=jnp.float32
            )
            dv_total += lax.dot_general(
                weights_low, grad_low, (((0,), (0,)), ((), ())), preferred_element_type=jnp.float32
            )
            if member == 0:
                pl.when(h + 2 < heads)(lambda: pass_clean(h + 2))
                pl.when(h >= 1)(lambda: pass_grads(h - 1))
            if member == 1:
                pl.when(h + 1 < heads)(lambda: pass_other(h + 1))
                pl.when(h >= 2)(lambda: pass_later(h - 2))
        dk_total = dk_total * (1.0 / LOG2E)
        for index in range(PIECES // 2):
            for part, total in enumerate((dk_total, dv_total)):
                at = 2 * index * piece_rows
                grad_own[h, index, part] = total[at : at + piece_rows]
                grad_out[h, index, part] = total[at + piece_rows : at + 2 * piece_rows].astype(
                    jnp.bfloat16
                )
        grad_pair(h).start()
        return carry

    lax.fori_loop(0, heads, step, 0)
    pass_grads(heads - 1)
    share(1, [jnp.sum(inner[at], axis=1, keepdims=True) for at in range(2)])
    for h in range(max(heads - 2, 0), heads):
        pass_later(h)
    totals = shared(1)
    norm_grad(grad_q_ref, raw_q, q_scaled, 0, totals[:, 0:1], q_width)
    norm_grad(grad_k_ref, raw_k, k_scaled, 1, totals[:, 1:2], key_width)
    for h in range(heads):
        finish(h)
    share(2, [jnp.sum(inner[2], axis=1, keepdims=True)])
    totals = shared(2)
    norm_grad(grad_ck_ref, raw_c, c_scaled, 2, totals[:, 0:1], key_width)
    for kind in kinds:
        for h in range(heads):
            kind(h).wait_send()
    for kind in range(3):
        for step_by in range(1, sides):
            stat_copy(kind, step_by).wait_send()


def on_device(
    noisy_q, noisy_k, noisy_value, clean_k, clean_value, q_gain, key_norm_gain, out_grad, window
):
    rows, width = noisy_q.shape
    assert STRETCH == 2 * rows
    heads = noisy_k.shape[1] // HEAD_SIZE
    sides = lax.axis_size("head")
    piece_rows = padded_rows(rows)
    key_rows = PIECES * piece_rows
    piece = pltpu.VMEM((heads, 2, piece_rows, HEAD_SIZE), jnp.bfloat16)
    triple = (heads, 3, 2, piece_rows, HEAD_SIZE)
    args = (
        window,
        noisy_q,
        noisy_k,
        noisy_value,
        clean_k,
        clean_value,
        q_gain[None, :],
        key_norm_gain[None, :],
        out_grad,
    )
    vmem = pl.BlockSpec(memory_space=pltpu.VMEM)
    wide = jax.ShapeDtypeStruct(noisy_q.shape, jnp.bfloat16)
    narrow = jax.ShapeDtypeStruct(noisy_k.shape, jnp.bfloat16)
    return pl.pallas_call(
        stretch_kernel,
        in_specs=[pl.BlockSpec(memory_space=pltpu.SMEM)] + [vmem] * (len(args) - 1),
        out_specs=[vmem] * 6,
        out_shape=[wide, wide, narrow, narrow, narrow, narrow],
        scratch_shapes=[piece] * 8
        + [
            pltpu.VMEM(triple, jnp.float32),
            pltpu.VMEM(triple, jnp.bfloat16),
            pltpu.VMEM(triple, jnp.bfloat16),
        ]
        + [piece] * 4
        + [
            pltpu.VMEM(noisy_q.shape, jnp.float32),
            pltpu.VMEM(noisy_k.shape, jnp.float32),
            pltpu.VMEM(noisy_k.shape, jnp.float32),
            pltpu.VMEM((3, rows, HEAD_SIZE), jnp.float32),
            pltpu.VMEM((3, rows, HEAD_SIZE), jnp.float32),
            pltpu.VMEM((1, key_rows), jnp.float32),
            pltpu.VMEM((1, HEAD_SIZE), jnp.float32),
            pltpu.VMEM((3, piece_rows, HEAD_SIZE), jnp.float32),
            pltpu.VMEM((3, max(sides - 1, 1), piece_rows, HEAD_SIZE), jnp.float32),
            pltpu.SemaphoreType.DMA((8, heads)),
            pltpu.SemaphoreType.DMA((8, heads)),
            pltpu.SemaphoreType.DMA((3, max(sides - 1, 1))),
            pltpu.SemaphoreType.DMA((3, max(sides - 1, 1))),
        ],
        compiler_params=pltpu.CompilerParams(
            collective_id=0, has_side_effects=True, vmem_limit_bytes=58 * 1024 * 1024
        ),
        cost_estimate=pl.CostEstimate(
            flops=2 * 6 * rows * GROUP * heads * key_rows * HEAD_SIZE,
            bytes_accessed=16 * 1024 * 1024,
            transcendentals=rows * GROUP * heads * key_rows,
        ),
    )(*args)


def solution(mesh):
    split = P("seq", "head")
    return jax.shard_map(
        on_device,
        mesh=mesh,
        in_specs=(split, split, split, split, split, P("head"), P("head"), split, P()),
        out_specs=(split,) * 6,
        check_vma=False,
    )
```

```python
import math

import jax
import jax.numpy as jnp
from jax import lax
from jax.experimental import pallas as pl
from jax.experimental.pallas import tpu as pltpu
from jax.sharding import PartitionSpec as P

HEAD_SIZE = 128
KEY_VALUE_HEADS = 8
GROUP = 3
STRETCH = 520
WINDOW = 3
SLOTS = 2
HQ = 24

EPSILON = 1e-06
NEG_FILL = -1e30
LOG2E = 1.0 / math.log(2.0)
PIECES = 6


def padded_rows(rows):
    return -(-rows // 16) * 16


def key_pieces(bufs, head, part):
    return jnp.concatenate([buf[head, part] for buf in bufs], axis=0)


def stretch_kernel(
    window,
    raw_q,
    raw_k,
    value,
    raw_c,
    clean_value,
    q_gain,
    key_gain,
    grad,
    out_ref,
    grad_q_ref,
    grad_k_ref,
    grad_v_ref,
    grad_ck_ref,
    grad_cv_ref,
    noisy_own,
    clean_own,
    noisy_par,
    prev_own,
    prev_par,
    relay,
    other_own,
    other_par,
    grad_own,
    grad_out,
    grad_in,
    later_out,
    later_in,
    next_out,
    next_in,
    q_scaled,
    k_scaled,
    c_scaled,
    inner,
    inverse_rms,
    bias,
    take_own,
    stat_out,
    stat_in,
    send_sems,
    recv_sems,
    stat_send,
    stat_recv,
):
    heads = noisy_own.shape[0]
    rows = raw_q.shape[0]
    piece_rows = noisy_own.shape[2]
    scale = HEAD_SIZE**-0.5
    here = lax.axis_index("seq")
    count = lax.axis_size("seq")
    partner = here + 1 - 2 * (here % 2)
    ahead = lambda steps: (here + 2 * steps) % count
    back = lambda steps: (here + count - 2 * steps) % count

    barrier = pltpu.get_barrier_semaphore()
    peers = (partner, ahead(1), ahead(2), back(1), back(2))
    for peer in peers:
        pl.semaphore_signal(
            barrier, inc=1, device_id={"seq": peer}, device_id_type=pl.DeviceIdType.MESH
        )
    side = lax.axis_index("head")
    sides = lax.axis_size("head")
    for step_by in range(1, sides):
        pl.semaphore_signal(
            barrier,
            inc=1,
            device_id={"head": (side + step_by) % sides},
            device_id_type=pl.DeviceIdType.MESH,
        )

    def stat_copy(kind, step_by):
        return pltpu.make_async_remote_copy(
            src_ref=stat_out.at[kind],
            dst_ref=stat_in.at[kind, step_by - 1],
            send_sem=stat_send.at[kind, step_by - 1],
            recv_sem=stat_recv.at[kind, step_by - 1],
            device_id={"head": (side + step_by) % sides},
            device_id_type=pl.DeviceIdType.MESH,
        )

    def share(kind, columns):
        lane = lax.broadcasted_iota(jnp.int32, (rows, HEAD_SIZE), 1)
        packed = jnp.zeros((rows, HEAD_SIZE), jnp.float32)
        for at, column in enumerate(columns):
            packed = jnp.where(lane == at, column, packed)
        stat_out[kind, :rows] = packed
        for step_by in range(1, sides):
            stat_copy(kind, step_by).start()

    def shared(kind):
        total = stat_out[kind]
        for step_by in range(1, sides):
            stat_copy(kind, step_by).wait_recv()
            total = total + stat_in[kind, step_by - 1]
        return total[:rows]

    def square_sum(ref):
        total = jnp.zeros((rows, HEAD_SIZE), jnp.float32)
        for first in range(0, ref.shape[1], HEAD_SIZE):
            full = ref[:, first : first + HEAD_SIZE].astype(jnp.float32)
            total = total + full * full
        return jnp.sum(total, axis=1, keepdims=True)

    q_width = HQ * HEAD_SIZE
    key_width = KEY_VALUE_HEADS * HEAD_SIZE
    stat_out[...] = jnp.zeros_like(stat_out)
    noisy_own[...] = jnp.zeros_like(noisy_own)
    clean_own[...] = jnp.zeros_like(clean_own)
    for h in range(heads):
        clean_own[h, 1, :rows] = clean_value[:, h * HEAD_SIZE : (h + 1) * HEAD_SIZE]
    square_sums = [square_sum(ref) for ref in (raw_q, raw_k, raw_c)]
    pl.semaphore_wait(barrier, len(peers) + sides - 1)
    share(0, square_sums)

    stretch_id = here // 2
    later_id = (stretch_id + 2) % window.shape[0]
    first_entry, second_entry = window[stretch_id, 0], window[stretch_id, 1]
    high = jnp.maximum(first_entry, second_entry)
    low = jnp.minimum(first_entry, second_entry)
    later_low = jnp.minimum(window[later_id, 0], window[later_id, 1])
    own_id = jnp.full((1, HEAD_SIZE), stretch_id, jnp.int32)
    take_own[...] = jnp.where(jnp.full((1, HEAD_SIZE), later_low) == own_id, 1.0, 0.0)
    lane = lax.broadcasted_iota(jnp.int32, bias.shape, 1)
    held = jnp.zeros(bias.shape, jnp.float32)
    for index in range(PIECES):
        at = index * piece_rows
        inside = jnp.where((lane >= at) & (lane < at + rows), 1.0, 0.0)
        if index >= 2:
            entry = jnp.full(bias.shape, high if index < 4 else low)
            inside = jnp.where(entry >= 0, inside, 0.0)
        held = held + inside
    bias[...] = jnp.where(held > 0.0, 0.0, NEG_FILL)
    inner[...] = jnp.zeros_like(inner)

    def copy(kind, head, src, dst, target, part=None):
        where = head if part is None else (head, part)
        return pltpu.make_async_remote_copy(
            src_ref=src.at[where],
            dst_ref=dst.at[where],
            send_sem=send_sems.at[kind, head],
            recv_sem=recv_sems.at[kind, head],
            device_id={"seq": target},
            device_id_type=pl.DeviceIdType.MESH,
        )

    key_next = lambda h: copy(0, h, clean_own, prev_own, ahead(1), 0)
    value_next = lambda h: copy(8, h, clean_own, prev_own, ahead(1), 1)
    noisy_pair = lambda h: copy(1, h, noisy_own, noisy_par, partner)
    prev_pair = lambda h: copy(2, h, prev_own, prev_par, partner)
    clean_later = lambda h: copy(3, h, relay, other_own, ahead(2))
    other_pair = lambda h: copy(4, h, other_own, other_par, partner)
    grad_pair = lambda h: copy(5, h, grad_out, grad_in, partner)
    grad_later = lambda h: copy(6, h, later_out, later_in, back(2))
    grad_next = lambda h: copy(7, h, next_out, next_in, back(1))
    stretches = window.shape[0]
    has_prev = stretch_id >= 1
    has_other = stretch_id >= 2
    has_next = stretch_id + 1 < stretches
    has_later = stretch_id + 2 < stretches

    @pl.when(has_next)
    def _():
        for h in range(min(2, heads)):
            value_next(h).start()

    @pl.when(jnp.logical_not(has_prev))
    def _():
        prev_own[...] = jnp.zeros_like(prev_own)

    @pl.when(jnp.logical_not(has_other))
    def _():
        other_own[...] = jnp.zeros_like(other_own)

    @pl.when(jnp.logical_not(has_next))
    def _():
        next_in[...] = jnp.zeros_like(next_in)

    @pl.when(jnp.logical_not(has_later))
    def _():
        later_in[...] = jnp.zeros_like(later_in)

    totals = shared(0)
    for at, width in enumerate((q_width, key_width, key_width)):
        mean = totals[:, at : at + 1] * (1.0 / width)
        inverse_rms[at] = jnp.broadcast_to(lax.rsqrt(mean + EPSILON), (rows, HEAD_SIZE))
    for h in range(heads):
        cols = slice(h * HEAD_SIZE, (h + 1) * HEAD_SIZE)
        gain_row = key_gain[cols].reshape(1, HEAD_SIZE)
        clean_own[h, 0, :rows] = (raw_c[:, cols].astype(jnp.float32) * inverse_rms[2] * gain_row).astype(
            jnp.bfloat16
        )
        if h < 2:
            pl.when(has_next)(key_next(h).start)
        noisy_own[h, 0, :rows] = (raw_k[:, cols].astype(jnp.float32) * inverse_rms[1] * gain_row).astype(
            jnp.bfloat16
        )
        noisy_own[h, 1, :rows] = value[:, cols]
        noisy_pair(h).start()

    def pass_clean(h):
        @pl.when(has_prev)
        def _():
            value_next(h).wait_recv()
            key_next(h).wait_recv()

        prev_pair(h).start()
        own = clean_own[h].astype(jnp.float32)
        prev = prev_own[h].astype(jnp.float32)
        relay[h] = jnp.where(take_own[...] > 0.0, own, prev).astype(jnp.bfloat16)
        pl.when(has_later)(clean_later(h).start)

    def pass_other(h):
        pl.when(has_other)(clean_later(h).wait_recv)
        other_pair(h).start()

    def pass_grads(h):
        grad_pair(h).wait_recv()
        later_out[h] = (grad_own[h, 2] + grad_in[h, 2].astype(jnp.float32)).astype(jnp.bfloat16)
        pl.when(has_other)(grad_later(h).start)
        cols = pl.ds(pl.multiple_of(h * HEAD_SIZE, HEAD_SIZE), HEAD_SIZE)
        total = grad_own[h, 0] + grad_in[h, 0].astype(jnp.float32)
        scaled = total[0, :rows] * key_gain[cols].reshape(1, HEAD_SIZE)
        k_scaled[:, cols] = scaled
        inner[1] += scaled * raw_k[:, cols].astype(jnp.float32)
        grad_v_ref[:, cols] = total[1, :rows].astype(jnp.bfloat16)
        grad_own[h, 1] = grad_own[h, 1] + grad_in[h, 1].astype(jnp.float32)

    def pass_later(h):
        pl.when(has_later)(grad_later(h).wait_recv)
        arrived = later_in[h].astype(jnp.float32)
        own = take_own[...] > 0.0
        next_out[h] = (grad_own[h, 1] + jnp.where(own, 0.0, arrived)).astype(jnp.bfloat16)
        pl.when(has_prev)(grad_next(h).start)

    def finish(h):
        pl.when(has_next)(grad_next(h).wait_recv)
        own = take_own[...] > 0.0
        total = next_in[h].astype(jnp.float32) + jnp.where(
            own, later_in[h].astype(jnp.float32), 0.0
        )
        cols = pl.ds(pl.multiple_of(h * HEAD_SIZE, HEAD_SIZE), HEAD_SIZE)
        scaled = total[0, :rows] * key_gain[cols].reshape(1, HEAD_SIZE)
        c_scaled[:, cols] = scaled
        inner[2] += scaled * raw_c[:, cols].astype(jnp.float32)
        grad_cv_ref[:, cols] = total[1, :rows].astype(jnp.bfloat16)

    def norm_grad(ref, raw, scaled, at, inner_sum, width):
        inv = inverse_rms[at]
        factor = inv * inv * inv * (inner_sum * (1.0 / width))
        for first in range(0, ref.shape[1], HEAD_SIZE):
            cols = slice(first, first + HEAD_SIZE)
            full = raw[:, cols].astype(jnp.float32)
            ref[:, cols] = (inv * scaled[:, cols] - full * factor).astype(ref.dtype)

    for h in range(min(2, heads)):
        pass_clean(h)
        if h + 2 < heads:
            pl.when(has_next)(value_next(h + 2).start)
            pl.when(has_next)(key_next(h + 2).start)
    pass_other(0)

    own_par = (noisy_own, noisy_par, prev_own, prev_par, other_own, other_par)

    def step(h, carry):
        noisy_pair(h).wait_recv()
        prev_pair(h).wait_recv()
        other_pair(h).wait_recv()
        keys = key_pieces(own_par, h, 0)
        values = key_pieces(own_par, h, 1)
        dk_total, dv_total = 0.0, 0.0
        for member in range(GROUP):
            first = pl.multiple_of((h * GROUP + member) * HEAD_SIZE, HEAD_SIZE)
            cols = pl.ds(first, HEAD_SIZE)
            gain_row = q_gain[cols].reshape(1, HEAD_SIZE) * (scale * LOG2E)
            query = (raw_q[:, cols].astype(jnp.float32) * inverse_rms[0] * gain_row).astype(
                jnp.bfloat16
            )
            scores = lax.dot_general(
                query, keys, (((1,), (1,)), ((), ())), preferred_element_type=jnp.float32
            )
            scores = scores + bias[...]
            row_max = jnp.max(scores, axis=1, keepdims=True)
            weights = jnp.exp2(scores - row_max)
            inverse = 1.0 / jnp.sum(weights, axis=1, keepdims=True)
            weights_low = weights.astype(jnp.bfloat16)
            head_out = jnp.dot(weights_low, values, preferred_element_type=jnp.float32) * inverse
            out_ref[:, cols] = head_out.astype(out_ref.dtype)
            grad_rows = grad[:, cols].astype(jnp.float32) * inverse
            delta = jnp.sum(grad_rows * head_out, axis=1, keepdims=True)
            grad_low = grad_rows.astype(jnp.bfloat16)
            dprobs = lax.dot_general(
                grad_low, values, (((1,), (1,)), ((), ())), preferred_element_type=jnp.float32
            )
            dscores = (weights * (dprobs - delta)).astype(jnp.bfloat16)
            dq = jnp.dot(dscores, keys, preferred_element_type=jnp.float32)
            scaled = dq * (q_gain[cols].reshape(1, HEAD_SIZE) * scale)
            q_scaled[:, cols] = scaled
            inner[0] += scaled * raw_q[:, cols].astype(jnp.float32)
            dk_total += lax.dot_general(
                dscores, query, (((0,), (0,)), ((), ())), preferred_element_type=jnp.float32
            )
            dv_total += lax.dot_general(
                weights_low, grad_low, (((0,), (0,)), ((), ())), preferred_element_type=jnp.float32
            )
            if member == 0:
                pl.when(h + 2 < heads)(lambda: pass_clean(h + 2))
                pl.when(h >= 1)(lambda: pass_grads(h - 1))
            if member == 1:
                pl.when(h + 1 < heads)(lambda: pass_other(h + 1))
                pl.when(h >= 2)(lambda: pass_later(h - 2))
        dk_total = dk_total * (1.0 / LOG2E)
        for index in range(PIECES // 2):
            for part, total in enumerate((dk_total, dv_total)):
                at = 2 * index * piece_rows
                grad_own[h, index, part] = total[at : at + piece_rows]
                grad_out[h, index, part] = total[at + piece_rows : at + 2 * piece_rows].astype(
                    jnp.bfloat16
                )
        grad_pair(h).start()
        return carry

    lax.fori_loop(0, heads, step, 0)
    pass_grads(heads - 1)
    share(1, [jnp.sum(inner[at], axis=1, keepdims=True) for at in range(2)])
    for h in range(max(heads - 2, 0), heads):
        pass_later(h)
    totals = shared(1)
    norm_grad(grad_q_ref, raw_q, q_scaled, 0, totals[:, 0:1], q_width)
    norm_grad(grad_k_ref, raw_k, k_scaled, 1, totals[:, 1:2], key_width)
    for h in range(heads):
        finish(h)
    share(2, [jnp.sum(inner[2], axis=1, keepdims=True)])
    totals = shared(2)
    norm_grad(grad_ck_ref, raw_c, c_scaled, 2, totals[:, 0:1], key_width)
    for h in range(heads):
        for kind in (noisy_pair, prev_pair, other_pair, grad_pair):
            kind(h).wait_send()

    def wait_sends(held, kinds):
        @pl.when(held)
        def _():
            for h in range(heads):
                for kind in kinds:
                    kind(h).wait_send()

    wait_sends(has_next, (value_next, key_next))
    wait_sends(has_later, (clean_later,))
    wait_sends(has_other, (grad_later,))
    wait_sends(has_prev, (grad_next,))
    for kind in range(3):
        for step_by in range(1, sides):
            stat_copy(kind, step_by).wait_send()


def hand_over_kernel(*refs):
    sems = refs[12]
    copies = [
        pltpu.make_async_copy(refs[at], refs[6 + at], sems.at[at]) for at in range(6)
    ]
    for copy in copies:
        copy.start()
    for copy in copies:
        copy.wait()


def on_device(
    noisy_q, noisy_k, noisy_value, clean_k, clean_value, q_gain, key_norm_gain, out_grad, window
):
    rows, width = noisy_q.shape
    assert STRETCH == 2 * rows
    heads = noisy_k.shape[1] // HEAD_SIZE
    sides = lax.axis_size("head")
    piece_rows = padded_rows(rows)
    key_rows = PIECES * piece_rows
    piece = pltpu.VMEM((heads, 2, piece_rows, HEAD_SIZE), jnp.bfloat16)
    triple = (heads, 3, 2, piece_rows, HEAD_SIZE)
    args = (
        window,
        noisy_q,
        noisy_k,
        noisy_value,
        clean_k,
        clean_value,
        q_gain,
        key_norm_gain,
        out_grad,
    )
    vmem = pl.BlockSpec(memory_space=pltpu.VMEM)
    wide = jax.ShapeDtypeStruct(noisy_q.shape, jnp.bfloat16)
    narrow = jax.ShapeDtypeStruct(noisy_k.shape, jnp.bfloat16)
    results = pl.pallas_call(
        stretch_kernel,
        in_specs=[pl.BlockSpec(memory_space=pltpu.SMEM)] + [vmem] * (len(args) - 1),
        out_specs=[vmem] * 6,
        out_shape=[wide, wide, narrow, narrow, narrow, narrow],
        scratch_shapes=[piece] * 8
        + [
            pltpu.VMEM(triple, jnp.float32),
            pltpu.VMEM(triple, jnp.bfloat16),
            pltpu.VMEM(triple, jnp.bfloat16),
        ]
        + [piece] * 4
        + [
            pltpu.VMEM(noisy_q.shape, jnp.float32),
            pltpu.VMEM(noisy_k.shape, jnp.float32),
            pltpu.VMEM(noisy_k.shape, jnp.float32),
            pltpu.VMEM((3, rows, HEAD_SIZE), jnp.float32),
            pltpu.VMEM((3, rows, HEAD_SIZE), jnp.float32),
            pltpu.VMEM((1, key_rows), jnp.float32),
            pltpu.VMEM((1, HEAD_SIZE), jnp.float32),
            pltpu.VMEM((3, piece_rows, HEAD_SIZE), jnp.float32),
            pltpu.VMEM((3, max(sides - 1, 1), piece_rows, HEAD_SIZE), jnp.float32),
            pltpu.SemaphoreType.DMA((9, heads)),
            pltpu.SemaphoreType.DMA((9, heads)),
            pltpu.SemaphoreType.DMA((3, max(sides - 1, 1))),
            pltpu.SemaphoreType.DMA((3, max(sides - 1, 1))),
        ],
        compiler_params=pltpu.CompilerParams(
            collective_id=0, has_side_effects=True, vmem_limit_bytes=58 * 1024 * 1024
        ),
        cost_estimate=pl.CostEstimate(
            flops=2 * 6 * rows * GROUP * heads * key_rows * HEAD_SIZE,
            bytes_accessed=16 * 1024 * 1024,
            transcendentals=rows * GROUP * heads * key_rows,
        ),
    )(*args)
    in_place = pl.BlockSpec(memory_space=pl.ANY)
    return pl.pallas_call(
        hand_over_kernel,
        in_specs=[in_place] * 6,
        out_specs=[in_place] * 6,
        out_shape=[wide, wide, narrow, narrow, narrow, narrow],
        scratch_shapes=[pltpu.SemaphoreType.DMA((6,))],
    )(*results)


def solution(mesh):
    split = P("seq", "head")
    return jax.shard_map(
        on_device,
        mesh=mesh,
        in_specs=(split, split, split, split, split, P("head"), P("head"), split, P()),
        out_specs=(split,) * 6,
        check_vma=False,
    )
```

```python
import math

import jax
import jax.numpy as jnp
from jax import lax
from jax.experimental import pallas as pl
from jax.experimental.pallas import tpu as pltpu
from jax.sharding import PartitionSpec as P

HEAD_SIZE = 128
KEY_VALUE_HEADS = 8
GROUP = 3
STRETCH = 520
WINDOW = 3
SLOTS = 2
HQ = 24

EPSILON = 1e-06
NEG_FILL = -1e30
LOG2E = 1.0 / math.log(2.0)
PIECES = 6


def padded_rows(rows):
    return -(-rows // 16) * 16


def key_pieces(bufs, head, part):
    return jnp.concatenate([buf[head, part] for buf in bufs], axis=0)


def stretch_kernel(
    window,
    raw_q,
    raw_k,
    value,
    raw_c,
    clean_value,
    q_gain,
    key_gain,
    grad,
    out_ref,
    grad_q_ref,
    grad_k_ref,
    grad_v_ref,
    grad_ck_ref,
    grad_cv_ref,
    noisy_own,
    clean_own,
    noisy_par,
    prev_own,
    prev_par,
    relay,
    other_own,
    other_par,
    grad_own,
    grad_out,
    grad_in,
    later_out,
    later_in,
    next_out,
    next_in,
    q_scaled,
    k_scaled,
    c_scaled,
    inner,
    inverse_rms,
    bias,
    take_own,
    all_dscores,
    all_weights,
    all_queries,
    all_grads,
    stat_out,
    stat_in,
    send_sems,
    recv_sems,
    stat_send,
    stat_recv,
):
    heads = noisy_own.shape[0]
    rows = raw_q.shape[0]
    piece_rows = noisy_own.shape[2]
    scale = HEAD_SIZE**-0.5
    here = lax.axis_index("seq")
    count = lax.axis_size("seq")
    partner = here + 1 - 2 * (here % 2)
    ahead = lambda steps: (here + 2 * steps) % count
    back = lambda steps: (here + count - 2 * steps) % count

    barrier = pltpu.get_barrier_semaphore()
    peers = (partner, ahead(1), ahead(2), back(1), back(2))
    for peer in peers:
        pl.semaphore_signal(
            barrier, inc=1, device_id={"seq": peer}, device_id_type=pl.DeviceIdType.MESH
        )
    side = lax.axis_index("head")
    sides = lax.axis_size("head")
    for step_by in range(1, sides):
        pl.semaphore_signal(
            barrier,
            inc=1,
            device_id={"head": (side + step_by) % sides},
            device_id_type=pl.DeviceIdType.MESH,
        )

    def stat_copy(kind, step_by):
        return pltpu.make_async_remote_copy(
            src_ref=stat_out.at[kind],
            dst_ref=stat_in.at[kind, step_by - 1],
            send_sem=stat_send.at[kind, step_by - 1],
            recv_sem=stat_recv.at[kind, step_by - 1],
            device_id={"head": (side + step_by) % sides},
            device_id_type=pl.DeviceIdType.MESH,
        )

    def share(kind, columns):
        lane = lax.broadcasted_iota(jnp.int32, (rows, HEAD_SIZE), 1)
        packed = jnp.zeros((rows, HEAD_SIZE), jnp.float32)
        for at, column in enumerate(columns):
            packed = jnp.where(lane == at, column, packed)
        stat_out[kind, :rows] = packed
        for step_by in range(1, sides):
            stat_copy(kind, step_by).start()

    def shared(kind):
        total = stat_out[kind]
        for step_by in range(1, sides):
            stat_copy(kind, step_by).wait_recv()
            total = total + stat_in[kind, step_by - 1]
        return total[:rows]

    def square_sum(ref):
        total = jnp.zeros((rows, HEAD_SIZE), jnp.float32)
        for first in range(0, ref.shape[1], HEAD_SIZE):
            full = ref[:, first : first + HEAD_SIZE].astype(jnp.float32)
            total = total + full * full
        return jnp.sum(total, axis=1, keepdims=True)

    q_width = HQ * HEAD_SIZE
    key_width = KEY_VALUE_HEADS * HEAD_SIZE
    stat_out[...] = jnp.zeros_like(stat_out)
    noisy_own[...] = jnp.zeros_like(noisy_own)
    clean_own[...] = jnp.zeros_like(clean_own)
    for h in range(heads):
        clean_own[h, 1, :rows] = clean_value[:, h * HEAD_SIZE : (h + 1) * HEAD_SIZE]
    square_sums = [square_sum(ref) for ref in (raw_q, raw_k, raw_c)]
    pl.semaphore_wait(barrier, len(peers) + sides - 1)
    share(0, square_sums)

    stretch_id = here // 2
    later_id = (stretch_id + 2) % window.shape[0]
    first_entry, second_entry = window[stretch_id, 0], window[stretch_id, 1]
    high = jnp.maximum(first_entry, second_entry)
    low = jnp.minimum(first_entry, second_entry)
    later_low = jnp.minimum(window[later_id, 0], window[later_id, 1])
    own_id = jnp.full((1, HEAD_SIZE), stretch_id, jnp.int32)
    take_own[...] = jnp.where(jnp.full((1, HEAD_SIZE), later_low) == own_id, 1.0, 0.0)
    lane = lax.broadcasted_iota(jnp.int32, bias.shape, 1)
    held = jnp.zeros(bias.shape, jnp.float32)
    for index in range(PIECES):
        at = index * piece_rows
        inside = jnp.where((lane >= at) & (lane < at + rows), 1.0, 0.0)
        if index >= 2:
            entry = jnp.full(bias.shape, high if index < 4 else low)
            inside = jnp.where(entry >= 0, inside, 0.0)
        held = held + inside
    bias[...] = jnp.where(held > 0.0, 0.0, NEG_FILL)
    inner[...] = jnp.zeros_like(inner)
    key_rows = bias.shape[1]
    for ref in (all_dscores, all_weights, all_queries, all_grads):
        for member in range(GROUP):
            end = (member + 1) * piece_rows
            ref[end - 16 : end] = jnp.zeros((16, ref.shape[1]), jnp.bfloat16)
    for ref in (all_dscores, all_weights):
        spare = ref.shape[1] - HEAD_SIZE
        ref[:, spare:] = jnp.zeros((ref.shape[0], HEAD_SIZE), jnp.bfloat16)

    def copy(kind, head, src, dst, target, part=None):
        where = head if part is None else (head, part)
        return pltpu.make_async_remote_copy(
            src_ref=src.at[where],
            dst_ref=dst.at[where],
            send_sem=send_sems.at[kind, head],
            recv_sem=recv_sems.at[kind, head],
            device_id={"seq": target},
            device_id_type=pl.DeviceIdType.MESH,
        )

    key_next = lambda h: copy(0, h, clean_own, prev_own, ahead(1), 0)
    value_next = lambda h: copy(8, h, clean_own, prev_own, ahead(1), 1)
    noisy_pair = lambda h: copy(1, h, noisy_own, noisy_par, partner)
    prev_pair = lambda h: copy(2, h, prev_own, prev_par, partner)
    clean_later = lambda h: copy(3, h, relay, other_own, ahead(2))
    other_pair = lambda h: copy(4, h, other_own, other_par, partner)
    grad_pair = lambda h: copy(5, h, grad_out, grad_in, partner)
    grad_later = lambda h: copy(6, h, later_out, later_in, back(2))
    grad_next = lambda h: copy(7, h, next_out, next_in, back(1))
    stretches = window.shape[0]
    has_prev = stretch_id >= 1
    has_other = stretch_id >= 2
    has_next = stretch_id + 1 < stretches
    has_later = stretch_id + 2 < stretches

    @pl.when(has_next)
    def _():
        for h in range(min(2, heads)):
            value_next(h).start()

    @pl.when(jnp.logical_not(has_prev))
    def _():
        prev_own[...] = jnp.zeros_like(prev_own)

    @pl.when(jnp.logical_not(has_other))
    def _():
        other_own[...] = jnp.zeros_like(other_own)

    @pl.when(jnp.logical_not(has_next))
    def _():
        next_in[...] = jnp.zeros_like(next_in)

    @pl.when(jnp.logical_not(has_later))
    def _():
        later_in[...] = jnp.zeros_like(later_in)

    totals = shared(0)
    for at, width in enumerate((q_width, key_width, key_width)):
        mean = totals[:, at : at + 1] * (1.0 / width)
        inverse_rms[at] = jnp.broadcast_to(lax.rsqrt(mean + EPSILON), (rows, HEAD_SIZE))
    for h in range(heads):
        cols = slice(h * HEAD_SIZE, (h + 1) * HEAD_SIZE)
        gain_row = key_gain[cols].reshape(1, HEAD_SIZE)
        clean_own[h, 0, :rows] = (raw_c[:, cols].astype(jnp.float32) * inverse_rms[2] * gain_row).astype(
            jnp.bfloat16
        )
        if h < 2:
            pl.when(has_next)(key_next(h).start)
        noisy_own[h, 0, :rows] = (raw_k[:, cols].astype(jnp.float32) * inverse_rms[1] * gain_row).astype(
            jnp.bfloat16
        )
        noisy_own[h, 1, :rows] = value[:, cols]
        noisy_pair(h).start()

    def pass_clean(h):
        @pl.when(has_prev)
        def _():
            value_next(h).wait_recv()
            key_next(h).wait_recv()

        prev_pair(h).start()
        own = clean_own[h].astype(jnp.float32)
        prev = prev_own[h].astype(jnp.float32)
        relay[h] = jnp.where(take_own[...] > 0.0, own, prev).astype(jnp.bfloat16)
        pl.when(has_later)(clean_later(h).start)

    def pass_other(h):
        pl.when(has_other)(clean_later(h).wait_recv)
        other_pair(h).start()

    def pass_grads(h):
        grad_pair(h).wait_recv()
        later_out[h] = (grad_own[h, 2] + grad_in[h, 2].astype(jnp.float32)).astype(jnp.bfloat16)
        pl.when(has_other)(grad_later(h).start)
        cols = pl.ds(pl.multiple_of(h * HEAD_SIZE, HEAD_SIZE), HEAD_SIZE)
        total = grad_own[h, 0] + grad_in[h, 0].astype(jnp.float32)
        scaled = total[0, :rows] * key_gain[cols].reshape(1, HEAD_SIZE)
        k_scaled[:, cols] = scaled
        inner[1] += scaled * raw_k[:, cols].astype(jnp.float32)
        grad_v_ref[:, cols] = total[1, :rows].astype(jnp.bfloat16)
        grad_own[h, 1] = grad_own[h, 1] + grad_in[h, 1].astype(jnp.float32)

    def pass_later(h):
        pl.when(has_later)(grad_later(h).wait_recv)
        arrived = later_in[h].astype(jnp.float32)
        own = take_own[...] > 0.0
        next_out[h] = (grad_own[h, 1] + jnp.where(own, 0.0, arrived)).astype(jnp.bfloat16)
        pl.when(has_prev)(grad_next(h).start)

    def finish(h):
        pl.when(has_next)(grad_next(h).wait_recv)
        own = take_own[...] > 0.0
        total = next_in[h].astype(jnp.float32) + jnp.where(
            own, later_in[h].astype(jnp.float32), 0.0
        )
        cols = pl.ds(pl.multiple_of(h * HEAD_SIZE, HEAD_SIZE), HEAD_SIZE)
        scaled = total[0, :rows] * key_gain[cols].reshape(1, HEAD_SIZE)
        c_scaled[:, cols] = scaled
        inner[2] += scaled * raw_c[:, cols].astype(jnp.float32)
        grad_cv_ref[:, cols] = total[1, :rows].astype(jnp.bfloat16)

    def norm_grad(ref, raw, scaled, at, inner_sum, width):
        inv = inverse_rms[at]
        factor = inv * inv * inv * (inner_sum * (1.0 / width))
        for first in range(0, ref.shape[1], HEAD_SIZE):
            cols = slice(first, first + HEAD_SIZE)
            full = raw[:, cols].astype(jnp.float32)
            ref[:, cols] = (inv * scaled[:, cols] - full * factor).astype(ref.dtype)

    for h in range(min(2, heads)):
        pass_clean(h)
        if h + 2 < heads:
            pl.when(has_next)(value_next(h + 2).start)
            pl.when(has_next)(key_next(h + 2).start)
    pass_other(0)

    own_par = (noisy_own, noisy_par, prev_own, prev_par, other_own, other_par)

    def step(h, carry):
        noisy_pair(h).wait_recv()
        prev_pair(h).wait_recv()
        other_pair(h).wait_recv()
        keys = key_pieces(own_par, h, 0)
        values = key_pieces(own_par, h, 1)
        for member in range(GROUP):
            first = pl.multiple_of((h * GROUP + member) * HEAD_SIZE, HEAD_SIZE)
            cols = pl.ds(first, HEAD_SIZE)
            gain_row = q_gain[cols].reshape(1, HEAD_SIZE) * (scale * LOG2E)
            query = (raw_q[:, cols].astype(jnp.float32) * inverse_rms[0] * gain_row).astype(
                jnp.bfloat16
            )
            scores = lax.dot_general(
                query, keys, (((1,), (1,)), ((), ())), preferred_element_type=jnp.float32
            )
            scores = scores + bias[...]
            row_max = jnp.max(scores, axis=1, keepdims=True)
            weights = jnp.exp2(scores - row_max)
            inverse = 1.0 / jnp.sum(weights, axis=1, keepdims=True)
            weights_low = weights.astype(jnp.bfloat16)
            head_out = jnp.dot(weights_low, values, preferred_element_type=jnp.float32) * inverse
            out_ref[:, cols] = head_out.astype(out_ref.dtype)
            grad_rows = grad[:, cols].astype(jnp.float32) * inverse
            delta = jnp.sum(grad_rows * head_out, axis=1, keepdims=True)
            grad_low = grad_rows.astype(jnp.bfloat16)
            dprobs = lax.dot_general(
                grad_low, values, (((1,), (1,)), ((), ())), preferred_element_type=jnp.float32
            )
            dscores = weights_low * (dprobs - delta).astype(jnp.bfloat16)
            dq = jnp.dot(dscores, keys, preferred_element_type=jnp.float32)
            scaled = dq * (q_gain[cols].reshape(1, HEAD_SIZE) * scale)
            q_scaled[:, cols] = scaled
            inner[0] += scaled * raw_q[:, cols].astype(jnp.float32)
            span = slice(member * piece_rows, member * piece_rows + rows)
            all_dscores[span, :key_rows] = dscores
            all_weights[span, :key_rows] = weights_low
            all_queries[span] = query
            all_grads[span] = grad_low
            if member == 0:
                pl.when(h + 2 < heads)(lambda: pass_clean(h + 2))
                pl.when(h >= 1)(lambda: pass_grads(h - 1))
                pl.when(h + 1 < heads)(lambda: pass_other(h + 1))
                pl.when(h >= 2)(lambda: pass_later(h - 2))

        def key_sums(small, large):
            across = lax.dot_general(
                small[...], large[...], (((0,), (0,)), ((), ())), preferred_element_type=jnp.float32
            )
            return across.T

        dk_total = key_sums(all_queries, all_dscores) * (1.0 / LOG2E)
        dv_total = key_sums(all_grads, all_weights)
        for index in range(PIECES // 2):
            for part, total in enumerate((dk_total, dv_total)):
                at = 2 * index * piece_rows
                grad_own[h, index, part] = total[at : at + piece_rows]
                grad_out[h, index, part] = total[at + piece_rows : at + 2 * piece_rows].astype(
                    jnp.bfloat16
                )
        grad_pair(h).start()
        return carry

    lax.fori_loop(0, heads, step, 0)
    pass_grads(heads - 1)
    share(1, [jnp.sum(inner[at], axis=1, keepdims=True) for at in range(2)])
    for h in range(max(heads - 2, 0), heads):
        pass_later(h)
    totals = shared(1)
    norm_grad(grad_q_ref, raw_q, q_scaled, 0, totals[:, 0:1], q_width)
    norm_grad(grad_k_ref, raw_k, k_scaled, 1, totals[:, 1:2], key_width)
    for h in range(heads):
        finish(h)
    share(2, [jnp.sum(inner[2], axis=1, keepdims=True)])
    totals = shared(2)
    norm_grad(grad_ck_ref, raw_c, c_scaled, 2, totals[:, 0:1], key_width)
    for h in range(heads):
        for kind in (noisy_pair, prev_pair, other_pair, grad_pair):
            kind(h).wait_send()

    def wait_sends(held, kinds):
        @pl.when(held)
        def _():
            for h in range(heads):
                for kind in kinds:
                    kind(h).wait_send()

    wait_sends(has_next, (value_next, key_next))
    wait_sends(has_later, (clean_later,))
    wait_sends(has_other, (grad_later,))
    wait_sends(has_prev, (grad_next,))
    for kind in range(3):
        for step_by in range(1, sides):
            stat_copy(kind, step_by).wait_send()


def hand_over_kernel(*refs):
    for at in range(6):
        refs[6 + at][...] = refs[at][...]


def on_device(
    noisy_q, noisy_k, noisy_value, clean_k, clean_value, q_gain, key_norm_gain, out_grad, window
):
    rows, width = noisy_q.shape
    assert STRETCH == 2 * rows
    heads = noisy_k.shape[1] // HEAD_SIZE
    sides = lax.axis_size("head")
    piece_rows = padded_rows(rows)
    key_rows = PIECES * piece_rows
    stacked = (GROUP * piece_rows, -(-key_rows // HEAD_SIZE) * HEAD_SIZE)
    piece = pltpu.VMEM((heads, 2, piece_rows, HEAD_SIZE), jnp.bfloat16)
    triple = (heads, 3, 2, piece_rows, HEAD_SIZE)
    args = (
        window,
        noisy_q,
        noisy_k,
        noisy_value,
        clean_k,
        clean_value,
        q_gain,
        key_norm_gain,
        out_grad,
    )
    vmem = pl.BlockSpec(memory_space=pltpu.VMEM)
    wide = jax.ShapeDtypeStruct(noisy_q.shape, jnp.bfloat16)
    narrow = jax.ShapeDtypeStruct(noisy_k.shape, jnp.bfloat16)
    results = pl.pallas_call(
        stretch_kernel,
        in_specs=[pl.BlockSpec(memory_space=pltpu.SMEM)] + [vmem] * (len(args) - 1),
        out_specs=[vmem] * 6,
        out_shape=[wide, wide, narrow, narrow, narrow, narrow],
        scratch_shapes=[piece] * 8
        + [
            pltpu.VMEM(triple, jnp.float32),
            pltpu.VMEM(triple, jnp.bfloat16),
            pltpu.VMEM(triple, jnp.bfloat16),
        ]
        + [piece] * 4
        + [
            pltpu.VMEM(noisy_q.shape, jnp.float32),
            pltpu.VMEM(noisy_k.shape, jnp.float32),
            pltpu.VMEM(noisy_k.shape, jnp.float32),
            pltpu.VMEM((3, rows, HEAD_SIZE), jnp.float32),
            pltpu.VMEM((3, rows, HEAD_SIZE), jnp.float32),
            pltpu.VMEM((1, key_rows), jnp.float32),
            pltpu.VMEM((1, HEAD_SIZE), jnp.float32),
            pltpu.VMEM(stacked, jnp.bfloat16),
            pltpu.VMEM(stacked, jnp.bfloat16),
            pltpu.VMEM((stacked[0], HEAD_SIZE), jnp.bfloat16),
            pltpu.VMEM((stacked[0], HEAD_SIZE), jnp.bfloat16),
            pltpu.VMEM((3, piece_rows, HEAD_SIZE), jnp.float32),
            pltpu.VMEM((3, max(sides - 1, 1), piece_rows, HEAD_SIZE), jnp.float32),
            pltpu.SemaphoreType.DMA((9, heads)),
            pltpu.SemaphoreType.DMA((9, heads)),
            pltpu.SemaphoreType.DMA((3, max(sides - 1, 1))),
            pltpu.SemaphoreType.DMA((3, max(sides - 1, 1))),
        ],
        compiler_params=pltpu.CompilerParams(
            collective_id=0, has_side_effects=True, vmem_limit_bytes=58 * 1024 * 1024
        ),
        cost_estimate=pl.CostEstimate(
            flops=2 * 6 * rows * GROUP * heads * key_rows * HEAD_SIZE,
            bytes_accessed=16 * 1024 * 1024,
            transcendentals=rows * GROUP * heads * key_rows,
        ),
    )(*args)
    blocks = [
        pl.BlockSpec((rows, array.shape[1] // heads), lambda j: (0, j)) for array in results
    ]
    return pl.pallas_call(
        hand_over_kernel,
        grid=(heads,),
        in_specs=blocks,
        out_specs=blocks,
        out_shape=[wide, wide, narrow, narrow, narrow, narrow],
    )(*results)


def solution(mesh):
    split = P("seq", "head")
    return jax.shard_map(
        on_device,
        mesh=mesh,
        in_specs=(split, split, split, split, split, P("head"), P("head"), split, P()),
        out_specs=(split,) * 6,
        check_vma=False,
    )
```

```python
import math

import jax
import jax.numpy as jnp
from jax import lax
from jax.experimental import pallas as pl
from jax.experimental.pallas import tpu as pltpu
from jax.sharding import PartitionSpec as P

HEAD_SIZE = 128
KEY_VALUE_HEADS = 8
GROUP = 3
STRETCH = 520
WINDOW = 3
SLOTS = 2
HQ = 24

EPSILON = 1e-06
NEG_FILL = -1e30
LOG2E = 1.0 / math.log(2.0)
PIECES = 6


def padded_rows(rows):
    return -(-rows // 16) * 16


def key_pieces(bufs, head, part):
    return jnp.concatenate([buf[head, part] for buf in bufs], axis=0)


def stretch_kernel(
    window,
    raw_q,
    raw_k,
    value,
    raw_c,
    clean_value,
    q_gain,
    key_gain,
    grad,
    out_ref,
    grad_q_ref,
    grad_k_ref,
    grad_v_ref,
    grad_ck_ref,
    grad_cv_ref,
    noisy_own,
    clean_own,
    noisy_par,
    prev_own,
    prev_par,
    relay,
    other_own,
    other_par,
    grad_own,
    grad_out,
    grad_in,
    later_out,
    later_in,
    next_out,
    next_in,
    q_scaled,
    k_scaled,
    c_scaled,
    inner,
    inverse_rms,
    bias,
    take_own,
    all_dscores,
    all_weights,
    all_queries,
    all_grads,
    stat_out,
    stat_in,
    send_sems,
    recv_sems,
    stat_send,
    stat_recv,
):
    heads = noisy_own.shape[0]
    rows = raw_q.shape[0]
    piece_rows = noisy_own.shape[2]
    scale = HEAD_SIZE**-0.5
    here = lax.axis_index("seq")
    count = lax.axis_size("seq")
    partner = here + 1 - 2 * (here % 2)
    ahead = lambda steps: (here + 2 * steps) % count
    back = lambda steps: (here + count - 2 * steps) % count

    barrier = pltpu.get_barrier_semaphore()
    peers = (partner, ahead(1), ahead(2), back(1), back(2))
    for peer in peers:
        pl.semaphore_signal(
            barrier, inc=1, device_id={"seq": peer}, device_id_type=pl.DeviceIdType.MESH
        )
    side = lax.axis_index("head")
    sides = lax.axis_size("head")
    for step_by in range(1, sides):
        pl.semaphore_signal(
            barrier,
            inc=1,
            device_id={"head": (side + step_by) % sides},
            device_id_type=pl.DeviceIdType.MESH,
        )

    def stat_copy(kind, step_by):
        return pltpu.make_async_remote_copy(
            src_ref=stat_out.at[kind],
            dst_ref=stat_in.at[kind, step_by - 1],
            send_sem=stat_send.at[kind, step_by - 1],
            recv_sem=stat_recv.at[kind, step_by - 1],
            device_id={"head": (side + step_by) % sides},
            device_id_type=pl.DeviceIdType.MESH,
        )

    def share(kind, columns):
        lane = lax.broadcasted_iota(jnp.int32, (rows, HEAD_SIZE), 1)
        packed = jnp.zeros((rows, HEAD_SIZE), jnp.float32)
        for at, column in enumerate(columns):
            packed = jnp.where(lane == at, column, packed)
        stat_out[kind, :rows] = packed
        for step_by in range(1, sides):
            stat_copy(kind, step_by).start()

    def shared(kind):
        total = stat_out[kind]
        for step_by in range(1, sides):
            stat_copy(kind, step_by).wait_recv()
            total = total + stat_in[kind, step_by - 1]
        return total[:rows]

    def square_sum(ref):
        total = jnp.zeros((rows, HEAD_SIZE), jnp.float32)
        for first in range(0, ref.shape[1], HEAD_SIZE):
            full = ref[:, first : first + HEAD_SIZE].astype(jnp.float32)
            total = total + full * full
        return jnp.sum(total, axis=1, keepdims=True)

    q_width = HQ * HEAD_SIZE
    key_width = KEY_VALUE_HEADS * HEAD_SIZE
    stat_out[...] = jnp.zeros_like(stat_out)
    noisy_own[...] = jnp.zeros_like(noisy_own)
    clean_own[...] = jnp.zeros_like(clean_own)
    for h in range(heads):
        clean_own[h, 1, :rows] = clean_value[:, h * HEAD_SIZE : (h + 1) * HEAD_SIZE]
    square_sums = [square_sum(ref) for ref in (raw_q, raw_k, raw_c)]
    pl.semaphore_wait(barrier, len(peers) + sides - 1)
    share(0, square_sums)

    stretch_id = here // 2
    later_id = (stretch_id + 2) % window.shape[0]
    first_entry, second_entry = window[stretch_id, 0], window[stretch_id, 1]
    high = jnp.maximum(first_entry, second_entry)
    low = jnp.minimum(first_entry, second_entry)
    later_low = jnp.minimum(window[later_id, 0], window[later_id, 1])
    own_id = jnp.full((1, HEAD_SIZE), stretch_id, jnp.int32)
    take_own[...] = jnp.where(jnp.full((1, HEAD_SIZE), later_low) == own_id, 1.0, 0.0)
    lane = lax.broadcasted_iota(jnp.int32, bias.shape, 1)
    held = jnp.zeros(bias.shape, jnp.float32)
    for index in range(PIECES):
        at = index * piece_rows
        inside = jnp.where((lane >= at) & (lane < at + rows), 1.0, 0.0)
        if index >= 2:
            entry = jnp.full(bias.shape, high if index < 4 else low)
            inside = jnp.where(entry >= 0, inside, 0.0)
        held = held + inside
    bias[...] = jnp.where(held > 0.0, 0.0, NEG_FILL)
    inner[...] = jnp.zeros_like(inner)
    key_rows = bias.shape[1]
    for ref in (all_dscores, all_weights, all_queries, all_grads):
        for member in range(GROUP):
            end = (member + 1) * piece_rows
            ref[end - 16 : end] = jnp.zeros((16, ref.shape[1]), jnp.bfloat16)
    for ref in (all_dscores, all_weights):
        spare = ref.shape[1] - HEAD_SIZE
        ref[:, spare:] = jnp.zeros((ref.shape[0], HEAD_SIZE), jnp.bfloat16)

    def copy(kind, head, part, src, dst, target, piece=None):
        where = (head, part) if piece is None else (head, piece, part)
        return pltpu.make_async_remote_copy(
            src_ref=src.at[where],
            dst_ref=dst.at[where],
            send_sem=send_sems.at[kind, head, part],
            recv_sem=recv_sems.at[kind, head, part],
            device_id={"seq": target},
            device_id_type=pl.DeviceIdType.MESH,
        )

    clean_next = lambda h, p: copy(0, h, p, clean_own, prev_own, ahead(1))
    noisy_pair = lambda h, p: copy(1, h, p, noisy_own, noisy_par, partner)
    prev_pair = lambda h, p: copy(2, h, p, prev_own, prev_par, partner)
    clean_later = lambda h, p: copy(3, h, p, relay, other_own, ahead(2))
    other_pair = lambda h, p: copy(4, h, p, other_own, other_par, partner)
    grad_later = lambda h, p: copy(5, h, p, later_out, later_in, back(2))
    grad_next = lambda h, p: copy(6, h, p, next_out, next_in, back(1))
    grad_noisy = lambda h, p: copy(7, h, p, grad_out, grad_in, partner, 0)
    grad_prev = lambda h, p: copy(8, h, p, grad_out, grad_in, partner, 1)
    grad_other = lambda h, p: copy(9, h, p, grad_out, grad_in, partner, 2)

    stretches = window.shape[0]
    has_prev = stretch_id >= 1
    has_other = stretch_id >= 2
    has_next = stretch_id + 1 < stretches
    has_later = stretch_id + 2 < stretches

    @pl.when(has_next)
    def _():
        for h in range(min(2, heads)):
            clean_next(h, 1).start()

    @pl.when(jnp.logical_not(has_prev))
    def _():
        prev_own[...] = jnp.zeros_like(prev_own)

    @pl.when(jnp.logical_not(has_other))
    def _():
        other_own[...] = jnp.zeros_like(other_own)

    @pl.when(jnp.logical_not(has_next))
    def _():
        next_in[...] = jnp.zeros_like(next_in)

    @pl.when(jnp.logical_not(has_later))
    def _():
        later_in[...] = jnp.zeros_like(later_in)

    totals = shared(0)
    for at, width in enumerate((q_width, key_width, key_width)):
        mean = totals[:, at : at + 1] * (1.0 / width)
        inverse_rms[at] = jnp.broadcast_to(lax.rsqrt(mean + EPSILON), (rows, HEAD_SIZE))
    for h in range(heads):
        cols = slice(h * HEAD_SIZE, (h + 1) * HEAD_SIZE)
        gain_row = key_gain[cols].reshape(1, HEAD_SIZE)
        clean_own[h, 0, :rows] = (raw_c[:, cols].astype(jnp.float32) * inverse_rms[2] * gain_row).astype(
            jnp.bfloat16
        )
        if h < 2:
            pl.when(has_next)(clean_next(h, 0).start)
        noisy_own[h, 0, :rows] = (raw_k[:, cols].astype(jnp.float32) * inverse_rms[1] * gain_row).astype(
            jnp.bfloat16
        )
        noisy_own[h, 1, :rows] = value[:, cols]
        for p in range(2):
            noisy_pair(h, p).start()

    def pass_clean(h):
        for p in (1, 0):
            pl.when(has_prev)(clean_next(h, p).wait_recv)
            own = clean_own[h, p].astype(jnp.float32)
            prev = prev_own[h, p].astype(jnp.float32)
            relay[h, p] = jnp.where(take_own[...] > 0.0, own, prev).astype(jnp.bfloat16)
            pl.when(has_later)(clean_later(h, p).start)
            prev_pair(h, p).start()

    def pass_other(h):
        for p in (1, 0):
            pl.when(has_other)(clean_later(h, p).wait_recv)
            other_pair(h, p).start()

    def pass_grads(h):
        for p in range(2):
            grad_other(h, p).wait_recv()
            later_out[h, p] = (grad_own[h, 2, p] + grad_in[h, 2, p].astype(jnp.float32)).astype(
                jnp.bfloat16
            )
            pl.when(has_other)(grad_later(h, p).start)
        for p in range(2):
            grad_prev(h, p).wait_recv()
            grad_own[h, 1, p] = grad_own[h, 1, p] + grad_in[h, 1, p].astype(jnp.float32)
        cols = pl.ds(pl.multiple_of(h * HEAD_SIZE, HEAD_SIZE), HEAD_SIZE)
        for p in range(2):
            grad_noisy(h, p).wait_recv()
            total = grad_own[h, 0, p] + grad_in[h, 0, p].astype(jnp.float32)
            if p == 0:
                scaled = total[:rows] * key_gain[cols].reshape(1, HEAD_SIZE)
                k_scaled[:, cols] = scaled
                inner[1] += scaled * raw_k[:, cols].astype(jnp.float32)
            else:
                grad_v_ref[:, cols] = total[:rows].astype(jnp.bfloat16)

    def pass_later(h):
        for p in range(2):
            pl.when(has_later)(grad_later(h, p).wait_recv)
            arrived = later_in[h, p].astype(jnp.float32)
            own = take_own[...] > 0.0
            next_out[h, p] = (grad_own[h, 1, p] + jnp.where(own, 0.0, arrived)).astype(
                jnp.bfloat16
            )
            pl.when(has_prev)(grad_next(h, p).start)

    def clean_total(h, p):
        pl.when(has_next)(grad_next(h, p).wait_recv)
        own = take_own[...] > 0.0
        arrived = later_in[h, p].astype(jnp.float32)
        return (next_in[h, p].astype(jnp.float32) + jnp.where(own, arrived, 0.0))[:rows]

    def finish_keys(h):
        cols = slice(h * HEAD_SIZE, (h + 1) * HEAD_SIZE)
        scaled = clean_total(h, 0) * key_gain[cols].reshape(1, HEAD_SIZE)
        c_scaled[:, cols] = scaled
        inner[2] += scaled * raw_c[:, cols].astype(jnp.float32)

    def finish_values(h):
        cols = slice(h * HEAD_SIZE, (h + 1) * HEAD_SIZE)
        grad_cv_ref[:, cols] = clean_total(h, 1).astype(jnp.bfloat16)

    def norm_grad(ref, raw, scaled, at, inner_sum, width):
        inv = inverse_rms[at]
        factor = inv * inv * inv * (inner_sum * (1.0 / width))
        for first in range(0, ref.shape[1], HEAD_SIZE):
            cols = slice(first, first + HEAD_SIZE)
            full = raw[:, cols].astype(jnp.float32)
            ref[:, cols] = (inv * scaled[:, cols] - full * factor).astype(ref.dtype)

    for h in range(min(2, heads)):
        pass_clean(h)
        if h + 2 < heads:
            for p in (1, 0):
                pl.when(has_next)(clean_next(h + 2, p).start)
    pass_other(0)

    own_par = (noisy_own, noisy_par, prev_own, prev_par, other_own, other_par)

    def step(h, carry):
        for p in range(2):
            noisy_pair(h, p).wait_recv()
            prev_pair(h, p).wait_recv()
            other_pair(h, p).wait_recv()
        keys = key_pieces(own_par, h, 0)
        values = key_pieces(own_par, h, 1)
        for member in range(GROUP):
            first = pl.multiple_of((h * GROUP + member) * HEAD_SIZE, HEAD_SIZE)
            cols = pl.ds(first, HEAD_SIZE)
            gain_row = q_gain[cols].reshape(1, HEAD_SIZE) * (scale * LOG2E)
            query = (raw_q[:, cols].astype(jnp.float32) * inverse_rms[0] * gain_row).astype(
                jnp.bfloat16
            )
            scores = lax.dot_general(
                query, keys, (((1,), (1,)), ((), ())), preferred_element_type=jnp.float32
            )
            scores = scores + bias[...]
            row_max = jnp.max(scores, axis=1, keepdims=True)
            weights = jnp.exp2(scores - row_max)
            inverse = 1.0 / jnp.sum(weights, axis=1, keepdims=True)
            weights_low = weights.astype(jnp.bfloat16)
            head_out = jnp.dot(weights_low, values, preferred_element_type=jnp.float32) * inverse
            out_ref[:, cols] = head_out.astype(out_ref.dtype)
            grad_rows = grad[:, cols].astype(jnp.float32) * inverse
            delta = jnp.sum(grad_rows * head_out, axis=1, keepdims=True)
            grad_low = grad_rows.astype(jnp.bfloat16)
            dprobs = lax.dot_general(
                grad_low, values, (((1,), (1,)), ((), ())), preferred_element_type=jnp.float32
            )
            dscores = weights_low * (dprobs - delta).astype(jnp.bfloat16)
            dq = jnp.dot(dscores, keys, preferred_element_type=jnp.float32)
            scaled = dq * (q_gain[cols].reshape(1, HEAD_SIZE) * scale)
            q_scaled[:, cols] = scaled
            inner[0] += scaled * raw_q[:, cols].astype(jnp.float32)
            span = slice(member * piece_rows, member * piece_rows + rows)
            all_dscores[span, :key_rows] = dscores
            all_weights[span, :key_rows] = weights_low
            all_queries[span] = query
            all_grads[span] = grad_low
            if member == 0:
                pl.when(h + 2 < heads)(lambda: pass_clean(h + 2))
                pl.when(h >= 1)(lambda: pass_grads(h - 1))
                pl.when(h + 1 < heads)(lambda: pass_other(h + 1))
                pl.when(h >= 2)(lambda: pass_later(h - 2))

        def key_sums(small, large):
            across = lax.dot_general(
                small[...], large[...], (((0,), (0,)), ((), ())), preferred_element_type=jnp.float32
            )
            return across.T

        for part in range(2):
            if part == 0:
                total = key_sums(all_queries, all_dscores) * (1.0 / LOG2E)
            else:
                total = key_sums(all_grads, all_weights)
            for index in (2, 1, 0):
                at = 2 * index * piece_rows
                grad_out[h, index, part] = total[at + piece_rows : at + 2 * piece_rows].astype(
                    jnp.bfloat16
                )
                (grad_noisy, grad_prev, grad_other)[index](h, part).start()
                grad_own[h, index, part] = total[at : at + piece_rows]
        return carry

    lax.fori_loop(0, heads, step, 0)
    for h in range(max(heads - 2, 0), heads - 1):
        pass_later(h)
    pass_grads(heads - 1)
    share(1, [jnp.sum(inner[at], axis=1, keepdims=True) for at in range(2)])
    for h in range(heads - 2):
        finish_keys(h)
    pass_later(heads - 1)
    totals = shared(1)
    norm_grad(grad_q_ref, raw_q, q_scaled, 0, totals[:, 0:1], q_width)
    norm_grad(grad_k_ref, raw_k, k_scaled, 1, totals[:, 1:2], key_width)
    for h in range(max(heads - 2, 0), heads):
        finish_keys(h)
    share(2, [jnp.sum(inner[2], axis=1, keepdims=True)])
    for h in range(heads):
        finish_values(h)
    totals = shared(2)
    norm_grad(grad_ck_ref, raw_c, c_scaled, 2, totals[:, 0:1], key_width)

    def wait_sends(copies):
        for h in range(heads):
            for p in range(2):
                for kind in copies:
                    kind(h, p).wait_send()

    wait_sends((noisy_pair, prev_pair, other_pair, grad_noisy, grad_prev, grad_other))
    pl.when(has_next)(lambda: wait_sends((clean_next,)))
    pl.when(has_later)(lambda: wait_sends((clean_later,)))
    pl.when(has_other)(lambda: wait_sends((grad_later,)))
    pl.when(has_prev)(lambda: wait_sends((grad_next,)))
    for kind in range(3):
        for step_by in range(1, sides):
            stat_copy(kind, step_by).wait_send()


def hand_over_kernel(*refs):
    for at in range(6):
        refs[6 + at][...] = refs[at][...]


def on_device(
    noisy_q, noisy_k, noisy_value, clean_k, clean_value, q_gain, key_norm_gain, out_grad, window
):
    rows, width = noisy_q.shape
    assert STRETCH == 2 * rows
    heads = noisy_k.shape[1] // HEAD_SIZE
    sides = lax.axis_size("head")
    piece_rows = padded_rows(rows)
    key_rows = PIECES * piece_rows
    stacked = (GROUP * piece_rows, -(-key_rows // HEAD_SIZE) * HEAD_SIZE)
    piece = pltpu.VMEM((heads, 2, piece_rows, HEAD_SIZE), jnp.bfloat16)
    triple = (heads, 3, 2, piece_rows, HEAD_SIZE)
    args = (
        window,
        noisy_q,
        noisy_k,
        noisy_value,
        clean_k,
        clean_value,
        q_gain,
        key_norm_gain,
        out_grad,
    )
    vmem = pl.BlockSpec(memory_space=pltpu.VMEM)
    wide = jax.ShapeDtypeStruct(noisy_q.shape, jnp.bfloat16)
    narrow = jax.ShapeDtypeStruct(noisy_k.shape, jnp.bfloat16)
    results = pl.pallas_call(
        stretch_kernel,
        in_specs=[pl.BlockSpec(memory_space=pltpu.SMEM)] + [vmem] * (len(args) - 1),
        out_specs=[vmem] * 6,
        out_shape=[wide, wide, narrow, narrow, narrow, narrow],
        scratch_shapes=[piece] * 8
        + [
            pltpu.VMEM(triple, jnp.float32),
            pltpu.VMEM(triple, jnp.bfloat16),
            pltpu.VMEM(triple, jnp.bfloat16),
        ]
        + [piece] * 4
        + [
            pltpu.VMEM(noisy_q.shape, jnp.float32),
            pltpu.VMEM(noisy_k.shape, jnp.float32),
            pltpu.VMEM(noisy_k.shape, jnp.float32),
            pltpu.VMEM((3, rows, HEAD_SIZE), jnp.float32),
            pltpu.VMEM((3, rows, HEAD_SIZE), jnp.float32),
            pltpu.VMEM((1, key_rows), jnp.float32),
            pltpu.VMEM((1, HEAD_SIZE), jnp.float32),
            pltpu.VMEM(stacked, jnp.bfloat16),
            pltpu.VMEM(stacked, jnp.bfloat16),
            pltpu.VMEM((stacked[0], HEAD_SIZE), jnp.bfloat16),
            pltpu.VMEM((stacked[0], HEAD_SIZE), jnp.bfloat16),
            pltpu.VMEM((3, piece_rows, HEAD_SIZE), jnp.float32),
            pltpu.VMEM((3, max(sides - 1, 1), piece_rows, HEAD_SIZE), jnp.float32),
            pltpu.SemaphoreType.DMA((10, heads, 2)),
            pltpu.SemaphoreType.DMA((10, heads, 2)),
            pltpu.SemaphoreType.DMA((3, max(sides - 1, 1))),
            pltpu.SemaphoreType.DMA((3, max(sides - 1, 1))),
        ],
        compiler_params=pltpu.CompilerParams(
            collective_id=0, has_side_effects=True, vmem_limit_bytes=58 * 1024 * 1024
        ),
        cost_estimate=pl.CostEstimate(
            flops=2 * 6 * rows * GROUP * heads * key_rows * HEAD_SIZE,
            bytes_accessed=16 * 1024 * 1024,
            transcendentals=rows * GROUP * heads * key_rows,
        ),
    )(*args)
    return pl.pallas_call(
        hand_over_kernel,
        in_specs=[vmem] * 6,
        out_specs=[vmem] * 6,
        out_shape=[wide, wide, narrow, narrow, narrow, narrow],
        compiler_params=pltpu.CompilerParams(vmem_limit_bytes=32 * 1024 * 1024),
    )(*results)


def solution(mesh):
    split = P("seq", "head")
    return jax.shard_map(
        on_device,
        mesh=mesh,
        in_specs=(split, split, split, split, split, P("head"), P("head"), split, P()),
        out_specs=(split,) * 6,
        check_vma=False,
    )
```

```python
import math

import jax
import jax.numpy as jnp
from jax import lax
from jax.experimental import pallas as pl
from jax.experimental.pallas import tpu as pltpu
from jax.sharding import PartitionSpec as P

HEAD_SIZE = 128
KEY_VALUE_HEADS = 8
GROUP = 3
STRETCH = 520
WINDOW = 3
SLOTS = 2
HQ = 24

EPSILON = 1e-06
NEG_FILL = -1e30
LOG2E = 1.0 / math.log(2.0)
PIECES = 6


def padded_rows(rows):
    return -(-rows // 16) * 16


def key_pieces(bufs, head, part):
    return jnp.concatenate([buf[head, part] for buf in bufs], axis=0)


def stretch_kernel(
    window,
    raw_q,
    raw_k,
    value,
    raw_c,
    clean_value,
    q_gain,
    key_gain,
    grad,
    out_ref,
    grad_q_ref,
    grad_k_ref,
    grad_v_ref,
    grad_ck_ref,
    grad_cv_ref,
    noisy_own,
    clean_own,
    noisy_par,
    prev_own,
    prev_par,
    relay,
    other_own,
    other_par,
    grad_own,
    grad_out,
    grad_in,
    later_out,
    later_in,
    next_out,
    next_in,
    q_scaled,
    k_scaled,
    c_scaled,
    inner,
    inverse_rms,
    bias,
    take_own,
    all_dscores,
    all_weights,
    all_queries,
    all_grads,
    stat_out,
    stat_in,
    send_sems,
    recv_sems,
    stat_send,
    stat_recv,
):
    heads = noisy_own.shape[0]
    rows = raw_q.shape[0]
    piece_rows = noisy_own.shape[2]
    scale = HEAD_SIZE**-0.5
    here = lax.axis_index("seq")
    count = lax.axis_size("seq")
    partner = here + 1 - 2 * (here % 2)
    ahead = lambda steps: (here + 2 * steps) % count
    back = lambda steps: (here + count - 2 * steps) % count

    barrier = pltpu.get_barrier_semaphore()
    peers = (partner, ahead(1), ahead(2), back(1), back(2))
    for peer in peers:
        pl.semaphore_signal(
            barrier, inc=1, device_id={"seq": peer}, device_id_type=pl.DeviceIdType.MESH
        )
    side = lax.axis_index("head")
    sides = lax.axis_size("head")
    for step_by in range(1, sides):
        pl.semaphore_signal(
            barrier,
            inc=1,
            device_id={"head": (side + step_by) % sides},
            device_id_type=pl.DeviceIdType.MESH,
        )

    def stat_copy(kind, step_by):
        return pltpu.make_async_remote_copy(
            src_ref=stat_out.at[kind],
            dst_ref=stat_in.at[kind, step_by - 1],
            send_sem=stat_send.at[kind, step_by - 1],
            recv_sem=stat_recv.at[kind, step_by - 1],
            device_id={"head": (side + step_by) % sides},
            device_id_type=pl.DeviceIdType.MESH,
        )

    def share(kind, columns):
        lane = lax.broadcasted_iota(jnp.int32, (rows, HEAD_SIZE), 1)
        packed = jnp.zeros((rows, HEAD_SIZE), jnp.float32)
        for at, column in enumerate(columns):
            packed = jnp.where(lane == at, column, packed)
        stat_out[kind, :rows] = packed
        for step_by in range(1, sides):
            stat_copy(kind, step_by).start()

    def shared(kind):
        total = stat_out[kind]
        for step_by in range(1, sides):
            stat_copy(kind, step_by).wait_recv()
            total = total + stat_in[kind, step_by - 1]
        return total[:rows]

    def square_sum(ref):
        total = jnp.zeros((rows, HEAD_SIZE), jnp.float32)
        for first in range(0, ref.shape[1], HEAD_SIZE):
            full = ref[:, first : first + HEAD_SIZE].astype(jnp.float32)
            total = total + full * full
        return jnp.sum(total, axis=1, keepdims=True)

    q_width = HQ * HEAD_SIZE
    key_width = KEY_VALUE_HEADS * HEAD_SIZE
    stat_out[...] = jnp.zeros_like(stat_out)
    noisy_own[...] = jnp.zeros_like(noisy_own)
    clean_own[...] = jnp.zeros_like(clean_own)
    for h in range(heads):
        clean_own[h, 1, :rows] = clean_value[:, h * HEAD_SIZE : (h + 1) * HEAD_SIZE]
    square_sums = [square_sum(ref) for ref in (raw_q, raw_k, raw_c)]
    pl.semaphore_wait(barrier, len(peers) + sides - 1)
    share(0, square_sums)

    stretch_id = here // 2
    later_id = (stretch_id + 2) % window.shape[0]
    first_entry, second_entry = window[stretch_id, 0], window[stretch_id, 1]
    high = jnp.maximum(first_entry, second_entry)
    low = jnp.minimum(first_entry, second_entry)
    later_low = jnp.minimum(window[later_id, 0], window[later_id, 1])
    own_id = jnp.full((1, HEAD_SIZE), stretch_id, jnp.int32)
    take_own[...] = jnp.where(jnp.full((1, HEAD_SIZE), later_low) == own_id, 1.0, 0.0)
    lane = lax.broadcasted_iota(jnp.int32, bias.shape, 1)
    held = jnp.zeros(bias.shape, jnp.float32)
    for index in range(PIECES):
        at = index * piece_rows
        inside = jnp.where((lane >= at) & (lane < at + rows), 1.0, 0.0)
        if index >= 2:
            entry = jnp.full(bias.shape, high if index < 4 else low)
            inside = jnp.where(entry >= 0, inside, 0.0)
        held = held + inside
    bias[...] = jnp.where(held > 0.0, 0.0, NEG_FILL)
    inner[...] = jnp.zeros_like(inner)
    key_rows = bias.shape[1]
    for ref in (all_dscores, all_weights, all_queries, all_grads):
        for member in range(GROUP):
            end = (member + 1) * piece_rows
            ref[end - 16 : end] = jnp.zeros((16, ref.shape[1]), jnp.bfloat16)
    for ref in (all_dscores, all_weights):
        spare = ref.shape[1] - HEAD_SIZE
        ref[:, spare:] = jnp.zeros((ref.shape[0], HEAD_SIZE), jnp.bfloat16)

    def copy(kind, head, part, src, dst, target, piece=None):
        where = (head, part) if piece is None else (head, piece, part)
        return pltpu.make_async_remote_copy(
            src_ref=src.at[where],
            dst_ref=dst.at[where],
            send_sem=send_sems.at[kind, head, part],
            recv_sem=recv_sems.at[kind, head, part],
            device_id={"seq": target},
            device_id_type=pl.DeviceIdType.MESH,
        )

    clean_next = lambda h, p: copy(0, h, p, clean_own, prev_own, ahead(1))
    noisy_pair = lambda h, p: copy(1, h, p, noisy_own, noisy_par, partner)
    prev_pair = lambda h, p: copy(2, h, p, prev_own, prev_par, partner)
    clean_later = lambda h, p: copy(3, h, p, relay, other_own, ahead(2))
    other_pair = lambda h, p: copy(4, h, p, other_own, other_par, partner)
    grad_later = lambda h, p: copy(5, h, p, later_out, later_in, back(2))
    grad_next = lambda h, p: copy(6, h, p, next_out, next_in, back(1))
    grad_noisy = lambda h, p: copy(7, h, p, grad_out, grad_in, partner, 0)
    grad_prev = lambda h, p: copy(8, h, p, grad_out, grad_in, partner, 1)
    grad_other = lambda h, p: copy(9, h, p, grad_out, grad_in, partner, 2)

    stretches = window.shape[0]
    has_prev = stretch_id >= 1
    has_other = stretch_id >= 2
    has_next = stretch_id + 1 < stretches
    has_later = stretch_id + 2 < stretches

    @pl.when(has_next)
    def _():
        for h in range(min(2, heads)):
            clean_next(h, 1).start()

    @pl.when(jnp.logical_not(has_prev))
    def _():
        prev_own[...] = jnp.zeros_like(prev_own)

    @pl.when(jnp.logical_not(has_other))
    def _():
        other_own[...] = jnp.zeros_like(other_own)

    @pl.when(jnp.logical_not(has_next))
    def _():
        next_in[...] = jnp.zeros_like(next_in)

    @pl.when(jnp.logical_not(has_later))
    def _():
        later_in[...] = jnp.zeros_like(later_in)

    totals = shared(0)
    for at, width in enumerate((q_width, key_width, key_width)):
        mean = totals[:, at : at + 1] * (1.0 / width)
        inverse_rms[at] = jnp.broadcast_to(lax.rsqrt(mean + EPSILON), (rows, HEAD_SIZE))
    for h in range(heads):
        cols = slice(h * HEAD_SIZE, (h + 1) * HEAD_SIZE)
        gain_row = key_gain[cols].reshape(1, HEAD_SIZE)
        clean_own[h, 0, :rows] = (raw_c[:, cols].astype(jnp.float32) * inverse_rms[2] * gain_row).astype(
            jnp.bfloat16
        )
        if h < 2:
            pl.when(has_next)(clean_next(h, 0).start)
        noisy_own[h, 0, :rows] = (raw_k[:, cols].astype(jnp.float32) * inverse_rms[1] * gain_row).astype(
            jnp.bfloat16
        )
        noisy_own[h, 1, :rows] = value[:, cols]
        for p in range(2):
            noisy_pair(h, p).start()

    def pass_clean(h):
        for p in (1, 0):
            pl.when(has_prev)(clean_next(h, p).wait_recv)
            own = clean_own[h, p].astype(jnp.float32)
            prev = prev_own[h, p].astype(jnp.float32)
            relay[h, p] = jnp.where(take_own[...] > 0.0, own, prev).astype(jnp.bfloat16)
            pl.when(has_later)(clean_later(h, p).start)
            prev_pair(h, p).start()

    def pass_other(h):
        for p in (1, 0):
            pl.when(has_other)(clean_later(h, p).wait_recv)
            other_pair(h, p).start()

    def pass_grads(h):
        for p in range(2):
            grad_other(h, p).wait_recv()
            later_out[h, p] = (grad_own[h, 2, p] + grad_in[h, 2, p].astype(jnp.float32)).astype(
                jnp.bfloat16
            )
            pl.when(has_other)(grad_later(h, p).start)
        for p in range(2):
            grad_prev(h, p).wait_recv()
            grad_own[h, 1, p] = grad_own[h, 1, p] + grad_in[h, 1, p].astype(jnp.float32)
        cols = pl.ds(pl.multiple_of(h * HEAD_SIZE, HEAD_SIZE), HEAD_SIZE)
        for p in range(2):
            grad_noisy(h, p).wait_recv()
            total = grad_own[h, 0, p] + grad_in[h, 0, p].astype(jnp.float32)
            if p == 0:
                scaled = total[:rows] * key_gain[cols].reshape(1, HEAD_SIZE)
                k_scaled[:, cols] = scaled
                inner[1] += scaled * raw_k[:, cols].astype(jnp.float32)
            else:
                grad_v_ref[:, cols] = total[:rows].astype(jnp.bfloat16)

    def pass_later(h):
        for p in range(2):
            pl.when(has_later)(grad_later(h, p).wait_recv)
            arrived = later_in[h, p].astype(jnp.float32)
            own = take_own[...] > 0.0
            next_out[h, p] = (grad_own[h, 1, p] + jnp.where(own, 0.0, arrived)).astype(
                jnp.bfloat16
            )
            pl.when(has_prev)(grad_next(h, p).start)

    def clean_total(h, p):
        pl.when(has_next)(grad_next(h, p).wait_recv)
        own = take_own[...] > 0.0
        arrived = later_in[h, p].astype(jnp.float32)
        return (next_in[h, p].astype(jnp.float32) + jnp.where(own, arrived, 0.0))[:rows]

    def finish_keys(h):
        cols = slice(h * HEAD_SIZE, (h + 1) * HEAD_SIZE)
        scaled = clean_total(h, 0) * key_gain[cols].reshape(1, HEAD_SIZE)
        c_scaled[:, cols] = scaled
        inner[2] += scaled * raw_c[:, cols].astype(jnp.float32)

    def finish_values(h):
        cols = slice(h * HEAD_SIZE, (h + 1) * HEAD_SIZE)
        grad_cv_ref[:, cols] = clean_total(h, 1).astype(jnp.bfloat16)

    def norm_grad(ref, raw, scaled, at, inner_sum, width):
        inv = inverse_rms[at]
        factor = inv * inv * inv * (inner_sum * (1.0 / width))
        for first in range(0, ref.shape[1], HEAD_SIZE):
            cols = slice(first, first + HEAD_SIZE)
            full = raw[:, cols].astype(jnp.float32)
            ref[:, cols] = (inv * scaled[:, cols] - full * factor).astype(ref.dtype)

    for h in range(min(2, heads)):
        pass_clean(h)
        if h + 2 < heads:
            for p in (1, 0):
                pl.when(has_next)(clean_next(h + 2, p).start)
    pass_other(0)

    own_par = (noisy_own, noisy_par, prev_own, prev_par, other_own, other_par)

    def step(h, carry):
        for p in range(2):
            noisy_pair(h, p).wait_recv()
            prev_pair(h, p).wait_recv()
            other_pair(h, p).wait_recv()
        keys = key_pieces(own_par, h, 0)
        values = key_pieces(own_par, h, 1)
        for member in range(GROUP):
            first = pl.multiple_of((h * GROUP + member) * HEAD_SIZE, HEAD_SIZE)
            cols = pl.ds(first, HEAD_SIZE)
            gain_row = q_gain[cols].reshape(1, HEAD_SIZE) * (scale * LOG2E)
            query = (raw_q[:, cols].astype(jnp.float32) * inverse_rms[0] * gain_row).astype(
                jnp.bfloat16
            )
            scores = lax.dot_general(
                query, keys, (((1,), (1,)), ((), ())), preferred_element_type=jnp.float32
            )
            scores = scores + bias[...]
            row_max = jnp.max(scores, axis=1, keepdims=True)
            weights = jnp.exp2(scores - row_max)
            inverse = 1.0 / jnp.sum(weights, axis=1, keepdims=True)
            weights_low = weights.astype(jnp.bfloat16)
            head_out = jnp.dot(weights_low, values, preferred_element_type=jnp.float32) * inverse
            out_ref[:, cols] = head_out.astype(out_ref.dtype)
            grad_rows = grad[:, cols].astype(jnp.float32) * inverse
            delta = jnp.sum(grad_rows * head_out, axis=1, keepdims=True)
            grad_low = grad_rows.astype(jnp.bfloat16)
            dprobs = lax.dot_general(
                grad_low, values, (((1,), (1,)), ((), ())), preferred_element_type=jnp.float32
            )
            dscores = weights_low * (dprobs - delta).astype(jnp.bfloat16)
            dq = jnp.dot(dscores, keys, preferred_element_type=jnp.float32)
            scaled = dq * (q_gain[cols].reshape(1, HEAD_SIZE) * scale)
            q_scaled[:, cols] = scaled
            inner[0] += scaled * raw_q[:, cols].astype(jnp.float32)
            span = slice(member * piece_rows, member * piece_rows + rows)
            all_dscores[span, :key_rows] = dscores
            all_weights[span, :key_rows] = weights_low
            all_queries[span] = query
            all_grads[span] = grad_low
            if member == 0:
                pl.when(h + 2 < heads)(lambda: pass_clean(h + 2))
                pl.when(h >= 1)(lambda: pass_grads(h - 1))
                pl.when(h + 1 < heads)(lambda: pass_other(h + 1))
                pl.when(h >= 2)(lambda: pass_later(h - 2))

        def key_sums(small, large):
            across = lax.dot_general(
                small[...], large[...], (((0,), (0,)), ((), ())), preferred_element_type=jnp.float32
            )
            return across.T

        for part in range(2):
            if part == 0:
                total = key_sums(all_queries, all_dscores) * (1.0 / LOG2E)
            else:
                total = key_sums(all_grads, all_weights)
            for index in (2, 1, 0):
                at = 2 * index * piece_rows
                grad_out[h, index, part] = total[at + piece_rows : at + 2 * piece_rows].astype(
                    jnp.bfloat16
                )
                (grad_noisy, grad_prev, grad_other)[index](h, part).start()
                grad_own[h, index, part] = total[at : at + piece_rows]
        return carry

    lax.fori_loop(0, heads, step, 0)
    for h in range(max(heads - 2, 0), heads - 1):
        pass_later(h)
    pass_grads(heads - 1)
    share(1, [jnp.sum(inner[at], axis=1, keepdims=True) for at in range(2)])
    for h in range(heads - 2):
        finish_keys(h)
    pass_later(heads - 1)
    totals = shared(1)
    norm_grad(grad_q_ref, raw_q, q_scaled, 0, totals[:, 0:1], q_width)
    norm_grad(grad_k_ref, raw_k, k_scaled, 1, totals[:, 1:2], key_width)
    for h in range(max(heads - 2, 0), heads):
        finish_keys(h)
    share(2, [jnp.sum(inner[2], axis=1, keepdims=True)])
    for h in range(heads):
        finish_values(h)
    totals = shared(2)
    norm_grad(grad_ck_ref, raw_c, c_scaled, 2, totals[:, 0:1], key_width)

    def wait_sends(copies):
        for h in range(heads):
            for p in range(2):
                for kind in copies:
                    kind(h, p).wait_send()

    wait_sends((noisy_pair, prev_pair, other_pair, grad_noisy, grad_prev, grad_other))
    pl.when(has_next)(lambda: wait_sends((clean_next,)))
    pl.when(has_later)(lambda: wait_sends((clean_later,)))
    pl.when(has_other)(lambda: wait_sends((grad_later,)))
    pl.when(has_prev)(lambda: wait_sends((grad_next,)))
    for kind in range(3):
        for step_by in range(1, sides):
            stat_copy(kind, step_by).wait_send()


def hand_over_kernel(*refs):
    for at in range(6):
        refs[6 + at][...] = refs[at][...]


def on_device(
    noisy_q, noisy_k, noisy_value, clean_k, clean_value, q_gain, key_norm_gain, out_grad, window
):
    rows, width = noisy_q.shape
    assert STRETCH == 2 * rows
    heads = noisy_k.shape[1] // HEAD_SIZE
    sides = lax.axis_size("head")
    piece_rows = padded_rows(rows)
    key_rows = PIECES * piece_rows
    stacked = (GROUP * piece_rows, -(-key_rows // HEAD_SIZE) * HEAD_SIZE)
    piece = pltpu.VMEM((heads, 2, piece_rows, HEAD_SIZE), jnp.bfloat16)
    triple = (heads, 3, 2, piece_rows, HEAD_SIZE)
    args = (
        window,
        noisy_q,
        noisy_k,
        noisy_value,
        clean_k,
        clean_value,
        q_gain,
        key_norm_gain,
        out_grad,
    )
    vmem = pl.BlockSpec(memory_space=pltpu.VMEM)
    wide = jax.ShapeDtypeStruct(noisy_q.shape, jnp.bfloat16)
    narrow = jax.ShapeDtypeStruct(noisy_k.shape, jnp.bfloat16)
    results = pl.pallas_call(
        stretch_kernel,
        in_specs=[pl.BlockSpec(memory_space=pltpu.SMEM)] + [vmem] * (len(args) - 1),
        out_specs=[vmem] * 6,
        out_shape=[wide, wide, narrow, narrow, narrow, narrow],
        scratch_shapes=[piece] * 8
        + [
            pltpu.VMEM(triple, jnp.float32),
            pltpu.VMEM(triple, jnp.bfloat16),
            pltpu.VMEM(triple, jnp.bfloat16),
        ]
        + [piece] * 4
        + [
            pltpu.VMEM(noisy_q.shape, jnp.float32),
            pltpu.VMEM(noisy_k.shape, jnp.float32),
            pltpu.VMEM(noisy_k.shape, jnp.float32),
            pltpu.VMEM((3, rows, HEAD_SIZE), jnp.float32),
            pltpu.VMEM((3, rows, HEAD_SIZE), jnp.float32),
            pltpu.VMEM((1, key_rows), jnp.float32),
            pltpu.VMEM((1, HEAD_SIZE), jnp.float32),
            pltpu.VMEM(stacked, jnp.bfloat16),
            pltpu.VMEM(stacked, jnp.bfloat16),
            pltpu.VMEM((stacked[0], HEAD_SIZE), jnp.bfloat16),
            pltpu.VMEM((stacked[0], HEAD_SIZE), jnp.bfloat16),
            pltpu.VMEM((3, piece_rows, HEAD_SIZE), jnp.float32),
            pltpu.VMEM((3, max(sides - 1, 1), piece_rows, HEAD_SIZE), jnp.float32),
            pltpu.SemaphoreType.DMA((10, heads, 2)),
            pltpu.SemaphoreType.DMA((10, heads, 2)),
            pltpu.SemaphoreType.DMA((3, max(sides - 1, 1))),
            pltpu.SemaphoreType.DMA((3, max(sides - 1, 1))),
        ],
        compiler_params=pltpu.CompilerParams(
            collective_id=0, has_side_effects=True, vmem_limit_bytes=58 * 1024 * 1024
        ),
        cost_estimate=pl.CostEstimate(
            flops=2 * 6 * rows * GROUP * heads * key_rows * HEAD_SIZE,
            bytes_accessed=16 * 1024 * 1024,
            transcendentals=rows * GROUP * heads * key_rows,
        ),
    )(*args)
    parts = 2 if heads % 2 == 0 else 1
    blocks = [
        pl.BlockSpec((rows, array.shape[1] // parts), lambda j: (0, j)) for array in results
    ]
    return pl.pallas_call(
        hand_over_kernel,
        grid=(parts,),
        in_specs=blocks,
        out_specs=blocks,
        out_shape=[wide, wide, narrow, narrow, narrow, narrow],
        compiler_params=pltpu.CompilerParams(vmem_limit_bytes=58 * 1024 * 1024),
    )(*results)


def solution(mesh):
    split = P("seq", "head")
    return jax.shard_map(
        on_device,
        mesh=mesh,
        in_specs=(split, split, split, split, split, P("head"), P("head"), split, P()),
        out_specs=(split,) * 6,
        check_vma=False,
    )
```
